768 devices in a mesh: path: 48 (over z, y_lo), shard: 16 (over y_hi, x, core).
Axes of the slice: x: 4, y: 8 (y_hi: 2, y_lo: 4; y = y_hi * 4 + y_lo), z: 12, core: 2. Of those that a mesh axis runs over, the one named last changes fastest.
Arguments:
- tokens: bfloat16 [9216, 2112], P('path'), may hold values from -6 to 6
- out_grad: bfloat16 [9216, 2112], P('path'), may hold values from -0.059814453 to 0.059814453
- doc_lengths: int32 [48, 24], P('path'), may hold values from 1 to 16, 192 in all within a row
- doc_paths: int32 [48, 24], P('path'), may hold values from 0 to 47
- membership: int32 [48, 2], replicated, may hold values from 0 to 3
- up_master: float32 [4, 2112, 8192], P(None, 'path', 'shard'), may hold values from -0.9574271 to 0.9574271
- down_master: float32 [4, 2112, 8192], P(None, 'path', 'shard'), may hold values from -0.4861359 to 0.4861359
- up_moment: bfloat16 [4, 2112, 8192], P(None, 'path', 'shard'), may hold values from -0.059814453 to 0.059814453
- down_moment: bfloat16 [4, 2112, 8192], P(None, 'path', 'shard'), may hold values from -0.059814453 to 0.059814453
Outputs:
- new_up_master: float32 [4, 2112, 8192], P(None, 'path', 'shard')
- new_down_master: float32 [4, 2112, 8192], P(None, 'path', 'shard')
- new_up_moment: bfloat16 [4, 2112, 8192], P(None, 'path', 'shard')
- new_down_moment: bfloat16 [4, 2112, 8192], P(None, 'path', 'shard')
The draws below stay inside these ranges and needn't reach their ends.
All inputs are finite; a program needn't handle non-finite values.
Results may differ from the reference program's by a relative error of at most 0.005.
The reference program's roundings to bfloat16 on the way (of `rows_in`, `grads_in`, `normed`, `hidden_b` and `dpre`) count: a program that leaves them out, or rounds other values in their place, can miss the bound.
Values may be sent and summed in bfloat16 or wider, within the bound.
A program may use at most 64 MiB of HBM per device.

```python
import math
import jax
import jax.numpy as jnp
import numpy as np
from jax import lax

D = 2112
FF = 8192
MODS = 4
DOCS = 24
TOK_DEV = 192
MOST = 16
PATHS = 48
CAP = 4
SLOTS = 192
ROWS = 9216


def ramped(key, fan_value, spread, wobble):
    first, second = jax.random.split(key)
    base = jax.random.truncated_normal(first, -4.0, 4.0, (MODS, D, FF), jnp.float32) / math.sqrt(fan_value)
    place = jnp.arange(FF, dtype=jnp.float32) / FF
    factor = jnp.exp(math.log(spread) * place) * jax.random.uniform(second, (FF,), jnp.float32, 1.0 / wobble, wobble)
    return base * factor * 0.8


def draw_up_master(key, part):
    key = jax.random.fold_in(key, 5)
    return ramped(key, D, 3.0, 1.3)


def draw_down_master(key, part):
    key = jax.random.fold_in(key, 9)
    return ramped(key, FF, 3.0, 1.3)


def place_ends(drawn, key, smallest, largest):
    spot = [jax.random.randint(jax.random.fold_in(key, axis), (), 0, length) for axis, length in enumerate(drawn.shape)]
    widest = drawn.shape.index(max(drawn.shape))
    neighbour = spot[:widest] + [(spot[widest] + 1) % drawn.shape[widest]] + spot[widest + 1:]
    return drawn.at[tuple(spot)].set(smallest).at[tuple(neighbour)].set(largest)


def steps_of(key, dims, cuts, least, top_value):
    loudness = 1.0
    for axis_at, blocks in cuts:
        draws = jax.random.uniform(jax.random.fold_in(jax.random.fold_in(key, 6), axis_at), (blocks,), jnp.float32, least / len(cuts), top_value / len(cuts))
        loudness = loudness * jnp.repeat(jnp.exp(draws), dims[axis_at] // blocks).reshape((-1,) + (1,) * (len(dims) - 1 - axis_at))
    return loudness


def cumulative_ranks(amount, skew):
    loads = [(1 << 20) // math.isqrt(grade ** skew) + 1 for grade in range(1, amount + 1)]
    scale = 1 + sum(loads) // (1 << 30)
    return np.cumsum(np.array([max(1, weight // scale) for weight in loads]))


def skewed_ids(own_key, dims, count, lean):
    grid = cumulative_ranks(count, lean)
    lot = jax.random.randint(jax.random.fold_in(own_key, 1), dims, 0, int(grid[count - 1]))
    rank = jnp.searchsorted(jnp.asarray(grid, jnp.int32), lot, side="right")
    return jax.random.permutation(jax.random.fold_in(own_key, 2), count)[rank].astype(jnp.int32)


def split_up(amount, total, most, lean):
    loads = [(1 << 20) // math.isqrt(standing ** lean) + 1 for standing in range(2, amount + 1)]
    rest, given = total - most - (amount - 1), [1] * (amount - 1)
    while rest > 0:
        candidates = [i for i in range(amount - 1) if given[i] < most]
        pool, remaining = sum([loads[i] for i in candidates]), rest
        for i in candidates:
            addition = min(most - given[i], max(1, remaining * loads[i] // pool), rest)
            given[i] = given[i] + addition
            rest = rest - addition
    return np.array([most] + given)


def ragged_sizes(key, number_of, total, bound, skew):
    if number_of == 2:
        one = jax.random.randint(key, (), max(1, total - bound), min(bound, total - 1) + 1)
        return jnp.stack([one, total - one])
    sizes = jnp.asarray(split_up(number_of, total, bound, skew), jnp.int32)
    twos = (number_of - 1) // 2
    giver, receiver = sizes[1:1 + 2 * twos:2], sizes[2:2 + 2 * twos:2]
    margin = jnp.minimum(giver - 1, bound - receiver)
    moved = jax.random.randint(jax.random.fold_in(key, 1), (twos,), 0, 1 << 20) % (margin + 1)
    sizes = sizes.at[1:1 + 2 * twos:2].set(giver - moved).at[2:2 + 2 * twos:2].set(receiver + moved)
    return sizes[jax.random.permutation(jax.random.fold_in(key, 2), number_of)]


def noise(rng, extent, width, bound, pieces=(), held_as=jnp.bfloat16):
    result = jax.random.normal(rng, extent, jnp.float32) * width
    if len(pieces) > 0:
        result = steps_of(rng, extent, pieces, -0.22, 0.18) * result
    return jnp.clip(result, min=-bound, max=bound).astype(held_as)


def setup_inputs(seed: int = 0) -> dict:
    streams_of = jax.random.split(jax.random.key(seed), 10)
    tokens = noise(streams_of[0], (ROWS, D), 1.0, 6.0, ((0, 48),))
    out_grad = noise(streams_of[1], (ROWS, D), 0.01, 0.059814453, ((0, 48),))
    doc_lengths = jax.vmap(lambda own: ragged_sizes(own, DOCS, TOK_DEV, MOST, 2))(jax.random.split(streams_of[2], PATHS)).reshape((PATHS, DOCS)).astype(jnp.int32)
    doc_paths = place_ends(skewed_ids(streams_of[3], (PATHS, DOCS), PATHS, 1), jax.random.fold_in(streams_of[3], 3), 0, PATHS - 1).astype(jnp.int32)
    membership = place_ends(jax.random.randint(streams_of[4], (PATHS, 2), 0, MODS), jax.random.fold_in(streams_of[4], 1), 0, MODS - 1).astype(jnp.int32)
    up_master = draw_up_master(jax.random.fold_in(streams_of[9], 71), 0)
    down_master = draw_down_master(jax.random.fold_in(streams_of[9], 71), 0)
    up_moment = noise(streams_of[7], (MODS, D, FF), 0.01, 0.059814453, ((1, 48), (2, 16)))
    down_moment = noise(streams_of[8], (MODS, D, FF), 0.01, 0.059814453, ((1, 48), (2, 16)))
    return {"tokens": tokens, "out_grad": out_grad, "doc_lengths": doc_lengths, "doc_paths": doc_paths, "membership": membership, "up_master": up_master, "down_master": down_master, "up_moment": up_moment, "down_moment": down_moment}


norm_epsilon = 1e-06
hidden_epsilon = 1e-05
adam_epsilon = 0.001
inner_rate = 0.05
decay_rate = 0.1
outer_rate = 0.7
momentum_coef = 0.9
gelu_coef = 0.7978845608
cubic_coef = 0.044715

def gelu_pair(values):
    inner = gelu_coef * (values + cubic_coef * values * values * values)
    tangent = jnp.tanh(inner)
    activated = 0.5 * values * (1.0 + tangent)
    slopes = 0.5 * (1.0 + tangent) + 0.5 * values * (1.0 - tangent * tangent) * gelu_coef * (1.0 + 3.0 * cubic_coef * values * values)
    return (activated, slopes)

def placing_matrix(lengths, targets, row_count, path_count, capacity):
    ends = jnp.cumsum(lengths)
    row_ids = jnp.arange(row_count, dtype=jnp.int32)
    doc_of_row = lax.optimization_barrier(jnp.sum((row_ids[:, None] >= ends[None, :]).astype(jnp.int32), axis=1))
    doc_hit = doc_of_row[:, None] == jnp.arange(lengths.shape[0], dtype=jnp.int32)[None, :]
    row_path = lax.optimization_barrier(jnp.sum(jnp.where(doc_hit, targets[None, :], 0), axis=1)).astype(jnp.int32)
    path_hit = (row_path[:, None] == jnp.arange(path_count, dtype=jnp.int32)[None, :]).astype(jnp.int32)
    ranks = lax.optimization_barrier(jnp.sum((jnp.cumsum(path_hit, axis=0) - 1) * path_hit, axis=1)).astype(jnp.int32)
    slots = jnp.where(ranks < capacity, row_path * capacity + ranks, -1)
    return (jnp.arange(path_count * capacity, dtype=jnp.int32)[:, None] == slots[None, :]).astype(jnp.bfloat16)

def adam_delta(gradient, weight):
    update = gradient / (jnp.abs(gradient) + adam_epsilon) + decay_rate * weight.astype(jnp.float32)
    return (-inner_rate * update).astype(jnp.bfloat16)

def outer_update(master, moment, summed, counts):
    pseudo = -summed / jnp.maximum(counts, 1.0)[:, None, None]
    buffer = momentum_coef * moment.astype(jnp.float32) + pseudo
    return (master - outer_rate * (pseudo + momentum_coef * buffer), buffer.astype(jnp.bfloat16))

def path_step(rows_in, grads_in, up_weight, down_weight):
    rows_float = rows_in.astype(jnp.float32)
    normed = (rows_float * lax.rsqrt(lax.optimization_barrier(jnp.mean(rows_float * rows_float, axis=1, keepdims=True)) + norm_epsilon)).astype(jnp.bfloat16)
    pre = jnp.dot(normed, up_weight, preferred_element_type=jnp.float32)
    activated, slopes = gelu_pair(pre)
    scale = jnp.sqrt(lax.optimization_barrier(jnp.mean(activated * activated, axis=1, keepdims=True)) + hidden_epsilon)
    hidden = activated / scale
    hidden_b = hidden.astype(jnp.bfloat16)
    grad_down = jnp.dot(grads_in.T, hidden_b, preferred_element_type=jnp.float32)
    back = jnp.dot(grads_in, down_weight, preferred_element_type=jnp.float32)
    mixing = lax.optimization_barrier(jnp.mean(back * hidden, axis=1, keepdims=True))
    dpre = ((back - hidden * mixing) / scale * slopes).astype(jnp.bfloat16)
    grad_up = jnp.dot(normed.T, dpre, preferred_element_type=jnp.float32)
    return (adam_delta(grad_up, up_weight), adam_delta(grad_down, down_weight))

def reference(tokens, out_grad, doc_lengths, doc_paths, membership, up_master, down_master, up_moment, down_moment):
    placing = jax.vmap(lambda lengths, targets: placing_matrix(lengths, targets, TOK_DEV, PATHS, CAP))(doc_lengths, doc_paths)
    placing_float = placing.astype(jnp.float32)
    token_groups = tokens.reshape(PATHS, TOK_DEV, D).astype(jnp.float32)
    grad_groups = out_grad.reshape(PATHS, TOK_DEV, D).astype(jnp.float32)
    sent_rows = jnp.einsum('gst,gtd->gsd', placing_float, token_groups).astype(jnp.bfloat16)
    sent_grads = jnp.einsum('gst,gtd->gsd', placing_float, grad_groups).astype(jnp.bfloat16)

    def visit(carry, path_id):
        sums_up, sums_down = carry
        start = (path_id * CAP).astype(jnp.int32)
        rows_in = lax.dynamic_slice_in_dim(sent_rows, start, CAP, 1).reshape(SLOTS, D)
        grads_in = lax.dynamic_slice_in_dim(sent_grads, start, CAP, 1).reshape(SLOTS, D)
        up_id = membership[path_id, 0]
        down_id = membership[path_id, 1]
        up_weight = up_master[up_id].astype(jnp.bfloat16)
        down_weight = down_master[down_id].astype(jnp.bfloat16)
        delta_up, delta_down = path_step(rows_in, grads_in, up_weight, down_weight)
        sums_up = sums_up.at[up_id].add(delta_up.astype(jnp.float32))
        sums_down = sums_down.at[down_id].add(delta_down.astype(jnp.float32))
        return ((sums_up, sums_down), None)
    zeros_sum = jnp.zeros((MODS, D, FF), jnp.float32)
    (sums_up, sums_down), unused = lax.scan(visit, (zeros_sum, zeros_sum), jnp.arange(PATHS, dtype=jnp.int32))
    module_ids = jnp.arange(MODS, dtype=jnp.int32)
    counts_up = lax.optimization_barrier(jnp.sum((membership[:, 0][None, :] == module_ids[:, None]).astype(jnp.float32), axis=1))
    counts_down = lax.optimization_barrier(jnp.sum((membership[:, 1][None, :] == module_ids[:, None]).astype(jnp.float32), axis=1))
    new_up_master, new_up_moment = outer_update(up_master, up_moment, sums_up, counts_up)
    new_down_master, new_down_moment = outer_update(down_master, down_moment, sums_down, counts_down)
    return (new_up_master, new_down_master, new_up_moment, new_down_moment)
```

```python
import functools

import jax
import jax.numpy as jnp
from jax import lax
from jax.experimental import pallas as pl
from jax.experimental.pallas import tpu as pltpu
from jax.sharding import PartitionSpec as P

MESH = pl.DeviceIdType.MESH
BF = jnp.bfloat16
F32 = jnp.float32

FF = 8192
NZ = 12
NYL = 4
NY = 8
NX = 4
UNIT = 16
HALF = 1152
OFFS = (0, -1, 1, -2, 2, -3, 3, -4)

norm_epsilon = 1e-06
hidden_epsilon = 1e-05
adam_epsilon = 0.001
inner_rate = 0.05
decay_rate = 0.1
outer_rate = 0.7
momentum_coef = 0.9
gelu_coef = 0.7978845608
cubic_coef = 0.044715


def gelu_pair(values):
    inner = gelu_coef * (values + cubic_coef * values * values * values)
    tangent = jnp.tanh(inner)
    activated = 0.5 * values * (1.0 + tangent)
    slopes = 0.5 * (1.0 + tangent) + 0.5 * values * (1.0 - tangent * tangent) * gelu_coef * (
        1.0 + 3.0 * cubic_coef * values * values
    )
    return (activated, slopes)


def placing_matrix(lengths, targets, row_count, path_count, capacity):
    ends = jnp.cumsum(lengths)
    row_ids = jnp.arange(row_count, dtype=jnp.int32)
    doc_of_row = jnp.sum((row_ids[:, None] >= ends[None, :]).astype(jnp.int32), axis=1)
    doc_hit = doc_of_row[:, None] == jnp.arange(lengths.shape[0], dtype=jnp.int32)[None, :]
    row_path = jnp.sum(jnp.where(doc_hit, targets[None, :], 0), axis=1)
    path_hit = (row_path[:, None] == jnp.arange(path_count, dtype=jnp.int32)[None, :]).astype(
        jnp.int32
    )
    ranks = jnp.sum((jnp.cumsum(path_hit, axis=0) - 1) * path_hit, axis=1)
    slots = jnp.where(ranks < capacity, row_path * capacity + ranks, -1)
    return (jnp.arange(path_count * capacity, dtype=jnp.int32)[:, None] == slots[None, :]).astype(
        jnp.bfloat16
    )


def adam_delta(gradient, weight):
    update = gradient / (jnp.abs(gradient) + adam_epsilon) + decay_rate * weight.astype(jnp.float32)
    return (-inner_rate * update).astype(jnp.bfloat16)


def outer_update(master, moment, summed, counts):
    pseudo = -summed / jnp.maximum(counts, 1.0)[:, None, None]
    buffer = momentum_coef * moment.astype(jnp.float32) + pseudo
    return (master - outer_rate * (pseudo + momentum_coef * buffer), buffer.astype(jnp.bfloat16))


def place():
    path = lax.axis_index("path")
    shard = lax.axis_index("shard")
    return path // NYL, path % NYL, shard // 8, (shard // 2) % NX, shard % 2


def device(z, y, x, core):
    return (z * NYL + y % NYL, ((y // NYL) * NX + x) * 2 + core)


def aligned(value, multiple):
    return pl.multiple_of(value, multiple)


def signal(to):
    pl.semaphore_signal(
        pltpu.get_barrier_semaphore(), inc=1, device_id=to, device_id_type=MESH
    )


def gather_kernel(
    rows_ref,
    wsend_ref,
    perm_ref,
    x_out,
    w_out,
    wrecv,
    unit,
    a_sem,
    e_sem,
    z_sem,
    y_sem,
    x_sem,
    f_sem,
    s_sem,
    l_sem,
):
    z, y_lo, y_hi, x, core = place()
    y = y_hi * NYL + y_lo
    row_block = aligned((x * NYL + y_lo) * 48, 16)

    def remote(src, dst, sems, to):
        return pltpu.make_async_remote_copy(
            src_ref=src,
            dst_ref=dst,
            send_sem=sems.at[0],
            recv_sem=sems.at[1],
            device_id=to,
            device_id_type=MESH,
        )

    def chunk(xx, yy):
        return x_out.at[
            core,
            pl.ds(aligned((xx * NYL + yy % NYL) * 48, 16), 48),
            pl.ds(aligned((yy // NYL) * HALF, 128), HALF),
        ]

    def slab(xx):
        return x_out.at[core, pl.ds(aligned(xx * 192, 16), 192), :]

    def wrows(level, zz, lanes):
        return w_out.at[level, pl.ds(aligned(zz * 176, 16), 176), lanes]

    x_right, x_left, x_far = (x + 1) % NX, (x + 3) % NX, (x + 2) % NX
    to_xr, to_xl = device(z, y, x_right, core), device(z, y, x_left, core)
    to_yr, to_yl = device(z, (y + 1) % NY, x, core), device(z, (y + 7) % NY, x, core)
    to_zr, to_zl = device((z + 1) % NZ, y, x, core), device((z + 11) % NZ, y, x, core)
    to_core = device(z, y, x, 1 - core)
    group = [y_hi * NYL + (y_lo + step) % NYL for step in (1, 2, 3)]

    for to in (to_xr, to_xl, to_yr, to_yl, to_zr, to_zl, to_core):
        signal(to)
    for other in group:
        signal(device(z, other, x, core))
    for j in (1, 2):
        signal(device((z + 2 * NZ - x - 4 * j) % NZ, y, x, core))

    signal(device((z + NZ - jnp.where(x == 0, 6, x)) % NZ, y, x, core))
    pl.semaphore_wait(pltpu.get_barrier_semaphore(), 13)

    trades = []
    for level in range(2):
        for step in (1, 2, 3):
            other = (y_lo + step) % NYL
            copy = remote(
                wsend_ref.at[level, other],
                wrecv.at[level, y_lo],
                e_sem.at[level, step - 1],
                device(z, y_hi * NYL + other, x, core),
            )
            copy.start()
            trades.append(copy)
        wrecv[level, y_lo] = wsend_ref[level, y_lo]

    routed = []
    for j in range(3):
        target = (z + x + 4 * j) % NZ
        routed.append(
            remote(
                rows_ref.at[pl.ds(aligned(target * UNIT, 16), UNIT), :],
                x_out.at[
                    core,
                    pl.ds(aligned(row_block + j * UNIT, 16), UNIT),
                    pl.ds(aligned(y_hi * HALF, 128), HALF),
                ],
                a_sem.at[j],
                device(target, y, x, core),
            )
        )
    routed[1].start()
    routed[2].start()

    @pl.when(x == 0)
    def _():
        pltpu.make_async_copy(
            rows_ref.at[pl.ds(aligned(z * UNIT, 16), UNIT), :],
            x_out.at[
                core,
                pl.ds(row_block, UNIT),
                pl.ds(aligned(y_hi * HALF, 128), HALF),
            ],
            l_sem.at[2],
        ).start()

    @pl.when(x != 0)
    def _():
        routed[0].start()

    every = slice(0, 512)
    zcopies = {}

    def z_send(level, t, lanes_right, lanes_left, src_unit):
        for side, (to, sign, lanes) in enumerate(
            ((to_zr, -1, lanes_right), (to_zl, 1, lanes_left))
        ):
            zz = (z + NZ + sign * t) % NZ
            dst = wrows(level, zz, lanes)
            copy = remote(unit.at[level] if src_unit else dst, dst, z_sem.at[level, t, side], to)
            copy.start()
            zcopies[level, t, side] = copy

    def z_step(level, t):
        zcopies[level, t - 1, 0].wait_recv()
        zcopies[level, t - 1, 1].wait_recv()
        if t < 5:
            z_send(level, t, every, every, False)
        else:
            z_send(level, t, slice(0, 256), slice(256, 512), False)

    locals_ = []
    for level in range(2):
        for copy in trades[3 * level : 3 * level + 3]:
            copy.wait_recv()
        pieces = wrecv[level].reshape(4 * 176, 128)
        for m in range(4):
            unit[level, :, m * 128 : (m + 1) * 128] = jnp.dot(
                perm_ref[m * 176 : (m + 1) * 176, :], pieces, preferred_element_type=F32
            ).astype(BF)
        z_send(level, 0, every, every, True)
        copy = pltpu.make_async_copy(unit.at[level], wrows(level, z, every), l_sem.at[level])
        copy.start()
        locals_.append(copy)

    routed[1].wait_recv()
    routed[2].wait_recv()

    @pl.when(x == 0)
    def _():
        pltpu.make_async_copy(
            rows_ref.at[pl.ds(aligned(z * UNIT, 16), UNIT), :],
            x_out.at[
                core,
                pl.ds(row_block, UNIT),
                pl.ds(aligned(y_hi * HALF, 128), HALF),
            ],
            l_sem.at[2],
        ).wait()

    @pl.when(x != 0)
    def _():
        routed[0].wait_recv()

    ycopies = {}
    xcopies = {}
    fcopies = {}
    scopies = []

    def y_send(t):
        for side, (to, sign) in enumerate(((to_yr, -1), (to_yl, 1))):
            if side == 1 and t == 3:
                continue
            ref = chunk(x, (y + NY + sign * t) % NY)
            copy = remote(ref, ref, y_sem.at[t, side], to)
            copy.start()
            ycopies[t, side] = copy

    def x_send(n):
        ref = chunk(x, (y + NY + OFFS[n]) % NY)
        for side, to in enumerate((to_xr, to_xl)):
            copy = remote(ref, ref, x_sem.at[n, side], to)
            copy.start()
            xcopies[n, side] = copy

    def x_forward(n):
        side = n % 2
        xcopies[n, side].wait_recv()
        ref = chunk(x_left if side == 0 else x_right, (y + NY + OFFS[n]) % NY)
        copy = remote(ref, ref, f_sem.at[n], to_xr if side == 0 else to_xl)
        copy.start()
        fcopies[n] = copy

    def core_send(index, xx):
        copy = remote(slab(xx), slab(xx), s_sem.at[index], to_core)
        copy.start()
        scopies.append(copy)

    y_send(0)
    x_send(0)
    for t in range(1, 4):
        ycopies[t - 1, 0].wait_recv()
        ycopies[t - 1, 1].wait_recv()
        y_send(t)
        x_send(2 * t - 1)
        x_send(2 * t)
        if t >= 2:
            z_step(t - 2, 1)
    ycopies[3, 0].wait_recv()
    x_send(7)
    core_send(0, x)
    for n in range(4):
        x_forward(n)
    z_step(0, 2)
    z_step(1, 2)
    for n in range(4, 8):
        x_forward(n)
    for n in range(8):
        xcopies[n, 1 - n % 2].wait_recv()
    core_send(1, x_left)
    core_send(2, x_right)
    z_step(0, 3)
    z_step(1, 3)
    for n in range(8):
        fcopies[n].wait_recv()
    core_send(3, x_far)
    for t in (4, 5):
        z_step(0, t)
        z_step(1, t)
    for copy in scopies:
        copy.wait_recv()
    for level in range(2):
        for side in range(2):
            zcopies[level, 5, side].wait_recv()

    for copy in trades + scopies:
        copy.wait_send()
    for copy in locals_:
        copy.wait()
    for table in (zcopies, ycopies, xcopies, fcopies):
        for copy in table.values():
            copy.wait_send()
    routed[1].wait_send()
    routed[2].wait_send()

    @pl.when(x != 0)
    def _():
        routed[0].wait_send()


def reduce_kernel(in_ref, out_ref, first, second, mid, a_sem, b_sem):
    z, y_lo, y_hi, x, core = place()
    y = y_hi * NYL + y_lo
    c = x * 2 + core
    ys = [(y + s) % NY for s in range(1, NY)]
    cs = [(c + s) % 8 for s in range(1, 8)]
    for other in ys:
        signal(device(z, other, x, core))
    for other in cs:
        signal(device(z, y, other // 2, other % 2))
    pl.semaphore_wait(pltpu.get_barrier_semaphore(), 14)

    def trade(src, slots, mine, sems, targets):
        copies = []
        for s, to in enumerate(targets):
            copy = pltpu.make_async_remote_copy(
                src_ref=src,
                dst_ref=slots.at[mine],
                send_sem=sems.at[s, 0],
                recv_sem=sems.at[s, 1],
                device_id=to,
                device_id_type=MESH,
            )
            copy.start()
            copies.append(copy)
        slots[mine] = src[...]
        for copy in copies:
            copy.wait_recv()
        total = slots[0]
        for i in range(1, 8):
            total += slots[i]
        return total, copies

    mid[...], one = trade(in_ref, first, y, a_sem, [device(z, o, x, core) for o in ys])
    out_ref[...], two = trade(
        mid, second, c, b_sem, [device(z, y, o // 2, o % 2) for o in cs]
    )
    for copy in one + two:
        copy.wait_send()


def ship_kernel(up_ref, down_ref, perm_ref, out_ref, recv, work, z_sem, e_sem):
    z, y_lo, y_hi, x, core = place()
    y = y_hi * NYL + y_lo
    to_z = (device((z + 1) % NZ, y, x, core), device((z + 11) % NZ, y, x, core))
    for to in to_z:
        signal(to)
    for step in (1, 2, 3):
        signal(device(z, y_hi * NYL + (y_lo + step) % NYL, x, core))
    pl.semaphore_wait(pltpu.get_barrier_semaphore(), 5)
    own = (up_ref, down_ref)
    halves = (slice(0, 256), slice(256, 512))
    copies = {}

    def send(src, level, t, side, lanes):
        copy = pltpu.make_async_remote_copy(
            src_ref=src,
            dst_ref=recv.at[level, side, t, :, lanes],
            send_sem=z_sem.at[level, t, side, 0],
            recv_sem=z_sem.at[level, t, side, 1],
            device_id=to_z[side],
            device_id_type=MESH,
        )
        copy.start()
        copies[level, t, side] = copy

    def rows(zz):
        return pl.ds(aligned(zz * 176, 16), 176)

    for level in range(2):
        for side in range(2):
            send(
                own[level].at[rows((z + 6) % NZ), halves[side]], level, 0, side, halves[side]
            )
    for t in range(1, 6):
        for level in range(2):
            for side in range(2):
                target = (z + (6 - t if side == 0 else NZ - 6 + t)) % NZ
                copies[level, t - 1, side].wait_recv()
                if t == 1:
                    lanes, rest = halves[side], halves[1 - side]
                    recv[level, side, 0, :, rest] = own[level][rows(target), rest]
                else:
                    lanes = slice(0, 512)
                recv[level, side, t - 1, :, lanes] = (
                    recv[level, side, t - 1, :, lanes].astype(F32)
                    + own[level][rows(target), lanes].astype(F32)
                ).astype(BF)
                send(recv.at[level, side, t - 1], level, t, side, slice(0, 512))

    trades = []
    for level in range(2):
        copies[level, 5, 0].wait_recv()
        copies[level, 5, 1].wait_recv()
        total = (
            own[level][rows(z), :].astype(F32)
            + recv[level, 0, 5].astype(F32)
            + recv[level, 1, 5].astype(F32)
        ).astype(BF)
        pieces = jnp.concatenate([total[:, m * 128 : (m + 1) * 128] for m in range(4)], axis=0)
        work[level] = (
            jnp.dot(perm_ref[...], pieces, preferred_element_type=F32)
            .astype(BF)
            .reshape(4, 176, 128)
        )
        for step in (1, 2, 3):
            other = (y_lo + step) % NYL
            copy = pltpu.make_async_remote_copy(
                src_ref=work.at[level, other],
                dst_ref=out_ref.at[level, y_lo],
                send_sem=e_sem.at[level, step - 1, 0],
                recv_sem=e_sem.at[level, step - 1, 1],
                device_id=device(z, y_hi * NYL + other, x, core),
                device_id_type=MESH,
            )
            copy.start()
            trades.append(copy)
        out_ref[level, y_lo] = work[level, y_lo]
    for copy in trades:
        copy.wait()
    for copy in copies.values():
        copy.wait_send()


VMEM = pl.BlockSpec(memory_space=pltpu.VMEM)
ANY = pl.BlockSpec(memory_space=pl.ANY)
DMA = pltpu.SemaphoreType.DMA


def gather(rows, weights, perm):
    return pl.pallas_call(
        gather_kernel,
        out_shape=(
            jax.ShapeDtypeStruct((2, 768, 2 * HALF), BF),
            jax.ShapeDtypeStruct((2, 2112, 512), BF),
        ),
        in_specs=[VMEM, VMEM, VMEM],
        out_specs=(ANY, ANY),
        scratch_shapes=[
            pltpu.VMEM((2, 4, 176, 128), BF),
            pltpu.VMEM((2, 176, 512), BF),
            DMA((3, 2)),
            DMA((2, 3, 2)),
            DMA((2, 6, 2, 2)),
            DMA((4, 2, 2)),
            DMA((8, 2, 2)),
            DMA((8, 2)),
            DMA((4, 2)),
            DMA((3,)),
        ],
        compiler_params=pltpu.CompilerParams(
            collective_id=0, has_side_effects=True, vmem_limit_bytes=48 * 1024 * 1024
        ),
        name="gather",
    )(rows, weights, perm)


def reduce_rows(sums):
    return pl.pallas_call(
        reduce_kernel,
        out_shape=jax.ShapeDtypeStruct((16, 128), F32),
        in_specs=[VMEM],
        out_specs=VMEM,
        scratch_shapes=[
            pltpu.VMEM((8, 16, 128), F32),
            pltpu.VMEM((8, 16, 128), F32),
            pltpu.VMEM((16, 128), F32),
            DMA((7, 2)),
            DMA((7, 2)),
        ],
        compiler_params=pltpu.CompilerParams(collective_id=1, has_side_effects=True),
        name="reduce_rows",
    )(sums)


def ship(up, down, perm):
    return pl.pallas_call(
        ship_kernel,
        out_shape=jax.ShapeDtypeStruct((2, 4, 176, 128), BF),
        in_specs=[VMEM, VMEM, VMEM],
        out_specs=VMEM,
        scratch_shapes=[
            pltpu.VMEM((2, 2, 6, 176, 512), BF),
            pltpu.VMEM((2, 4, 176, 128), BF),
            DMA((2, 6, 2, 2)),
            DMA((2, 3, 2)),
        ],
        compiler_params=pltpu.CompilerParams(
            collective_id=2, has_side_effects=True, vmem_limit_bytes=48 * 1024 * 1024
        ),
        name="ship",
    )(up, down, perm)


def on_device(
    tokens,
    out_grad,
    doc_lengths,
    doc_paths,
    membership,
    up_master,
    down_master,
    up_moment,
    down_moment,
):
    path_count = lax.axis_size("path")
    row_count, width = tokens.shape
    module_count, owner_rows, owner_columns = up_master.shape
    capacity = row_count // path_count
    z, y_lo, y_hi, x, core = place()

    placing = placing_matrix(doc_lengths[0], doc_paths[0], row_count, path_count, capacity)
    rows_float = tokens.astype(F32)
    normed = (
        rows_float
        * lax.rsqrt(jnp.mean(rows_float * rows_float, axis=1, keepdims=True) + norm_epsilon)
    ).astype(BF)
    chosen = jnp.where(core == 0, normed, out_grad)
    half = jnp.where(
        y_hi == 0,
        chosen[:, :HALF],
        jnp.pad(chosen[:, HALF:], ((0, 0), (0, 2 * HALF - width))),
    )
    rows = jnp.dot(placing, half, preferred_element_type=F32).astype(BF)

    def blocks(master):
        flat = master.astype(BF).reshape(module_count * owner_rows, NYL, 128)
        return flat.transpose(1, 0, 2)

    weights_out = jnp.stack([blocks(up_master), blocks(down_master)])
    index = jnp.arange(NYL * module_count * owner_rows, dtype=jnp.int32)
    m_of = index // (NYL * owner_rows)
    y_of = (index // owner_rows) % NYL
    source = (y_of * module_count + m_of) * owner_rows + index % owner_rows
    perm = (source[:, None] == index[None, :]).astype(BF)

    features, weights = gather(rows, weights_out, perm)
    normed_in = features[0, :, :width]
    grads_in = features[1, :, :width]
    up_weight, down_weight = weights[0], weights[1]

    plane_rows = features.shape[1]
    row_path = (jnp.arange(plane_rows, dtype=jnp.int32) // capacity) % NYL
    members = lax.dynamic_slice_in_dim(membership, z * NYL, NYL, 0)
    row_hit = row_path[:, None] == jnp.arange(NYL, dtype=jnp.int32)[None, :]
    row_module = jnp.sum(
        jnp.where(row_hit[:, :, None], members[None, :, :], 0), axis=1
    )

    def pick(product, level):
        out = 0.0
        for m in range(module_count):
            out = jnp.where(
                row_module[:, level : level + 1] == m, product[:, m * 128 : (m + 1) * 128], out
            )
        return out

    pre = pick(jnp.dot(normed_in, up_weight, preferred_element_type=F32), 0)
    back = pick(jnp.dot(grads_in, down_weight, preferred_element_type=F32), 1)
    activated, slopes = gelu_pair(pre)
    squares = jnp.sum(activated * activated, axis=1)
    products = jnp.sum(back * activated, axis=1)
    sums = jnp.concatenate(
        [squares.reshape(6, 128), products.reshape(6, 128), jnp.zeros((4, 128), F32)], axis=0
    )
    sums = reduce_rows(sums)
    scale = jnp.sqrt(sums[:6].reshape(plane_rows) / FF + hidden_epsilon)[:, None]
    mixing = sums[6:12].reshape(plane_rows)[:, None] / scale / FF
    hidden = activated / scale
    hidden_b = hidden.astype(BF)
    dpre = ((back - hidden * mixing) / scale * slopes).astype(BF)

    def spread(values):
        return jnp.concatenate(
            [jnp.where(row_hit[:, i : i + 1], values, 0) for i in range(NYL)], axis=1
        )

    def module_sums(left, right, weight, level):
        gradient = lax.dot_general(
            left, spread(right), (((0,), (0,)), ((), ())), preferred_element_type=F32
        )
        totals = [jnp.zeros((width, 128), F32) for _ in range(module_count)]
        for i in range(NYL):
            mine = weight[:, :128]
            for m in range(1, module_count):
                mine = jnp.where(members[i, level] == m, weight[:, m * 128 : (m + 1) * 128], mine)
            delta = adam_delta(gradient[:, i * 128 : (i + 1) * 128], mine).astype(F32)
            for m in range(module_count):
                totals[m] = totals[m] + jnp.where(members[i, level] == m, delta, 0.0)
        return jnp.concatenate(totals, axis=1).astype(BF)

    down_sums = module_sums(grads_in, hidden_b, down_weight, 1)
    up_sums = module_sums(normed_in, dpre, up_weight, 0)
    summed = ship(up_sums, down_sums, perm.T)

    module_ids = jnp.arange(module_count, dtype=jnp.int32)

    def update(master, moment, level):
        counts = jnp.sum((membership[:, level][None, :] == module_ids[:, None]).astype(F32), axis=1)
        total = (
            summed[level]
            .reshape(NYL, module_count, owner_rows, 128)
            .transpose(1, 2, 0, 3)
            .reshape(module_count, owner_rows, owner_columns)
        )
        return outer_update(master, moment, total.astype(F32), counts)

    new_up, new_up_moment = update(up_master, up_moment, 0)
    new_down, new_down_moment = update(down_master, down_moment, 1)
    return (new_up, new_down, new_up_moment, new_down_moment)


def solution(mesh):
    split = P(None, "path", "shard")
    rows = P("path", None)
    return jax.shard_map(
        on_device,
        mesh=mesh,
        in_specs=(rows, rows, rows, rows, P(), split, split, split, split),
        out_specs=(split, split, split, split),
        check_vma=False,
    )
```

```python
import functools

import jax
import jax.numpy as jnp
from jax import lax
from jax.experimental import pallas as pl
from jax.experimental.pallas import tpu as pltpu
from jax.sharding import PartitionSpec as P

MESH = pl.DeviceIdType.MESH
BF = jnp.bfloat16
F32 = jnp.float32

FF = 8192
NZ = 12
NYL = 4
NY = 8
NX = 4
UNIT = 16
HALF = 1152
WIDE = 2304
BLOCK = 192
USED = 176
PLANE = 768
OFFS = (0, -1, 1, -2, 2, -3, 3, -4)

norm_epsilon = 1e-06
hidden_epsilon = 1e-05
adam_epsilon = 0.001
inner_rate = 0.05
decay_rate = 0.1
outer_rate = 0.7
momentum_coef = 0.9
gelu_coef = 0.7978845608
cubic_coef = 0.044715


def gelu_pair(values):
    inner = gelu_coef * (values + cubic_coef * values * values * values)
    tangent = jnp.tanh(inner)
    activated = 0.5 * values * (1.0 + tangent)
    slopes = 0.5 * (1.0 + tangent) + 0.5 * values * (1.0 - tangent * tangent) * gelu_coef * (
        1.0 + 3.0 * cubic_coef * values * values
    )
    return (activated, slopes)


def placing_matrix(lengths, targets, row_count, path_count, capacity):
    ends = jnp.cumsum(lengths)
    row_ids = jnp.arange(row_count, dtype=jnp.int32)
    doc_of_row = jnp.sum((row_ids[:, None] >= ends[None, :]).astype(jnp.int32), axis=1)
    doc_hit = doc_of_row[:, None] == jnp.arange(lengths.shape[0], dtype=jnp.int32)[None, :]
    row_path = jnp.sum(jnp.where(doc_hit, targets[None, :], 0), axis=1)
    path_hit = (row_path[:, None] == jnp.arange(path_count, dtype=jnp.int32)[None, :]).astype(
        jnp.int32
    )
    ranks = jnp.sum((jnp.cumsum(path_hit, axis=0) - 1) * path_hit, axis=1)
    slots = jnp.where(ranks < capacity, row_path * capacity + ranks, -1)
    return (jnp.arange(path_count * capacity, dtype=jnp.int32)[:, None] == slots[None, :]).astype(
        jnp.bfloat16
    )


def adam_delta(gradient, weight):
    update = gradient / (jnp.abs(gradient) + adam_epsilon) + decay_rate * weight.astype(jnp.float32)
    return (-inner_rate * update).astype(jnp.bfloat16)


def outer_update(master, moment, summed, counts):
    pseudo = -summed / jnp.maximum(counts, 1.0)[:, None, None]
    buffer = momentum_coef * moment.astype(jnp.float32) + pseudo
    return (master - outer_rate * (pseudo + momentum_coef * buffer), buffer.astype(jnp.bfloat16))


def place():
    path = lax.axis_index("path")
    shard = lax.axis_index("shard")
    return path // NYL, path % NYL, shard // 8, (shard // 2) % NX, shard % 2


def device(z, y, x, core):
    return (z * NYL + y % NYL, ((y // NYL) * NX + x) * 2 + core)


def aligned(value, multiple):
    return pl.multiple_of(value, multiple)


def signal(to):
    pl.semaphore_signal(
        pltpu.get_barrier_semaphore(), inc=1, device_id=to, device_id_type=MESH
    )


def fused_kernel(
    rows_ref,
    wsend_ref,
    mask_ref,
    pick_ref,
    out_ref,
    xs,
    xt,
    up_w,
    down_w,
    grads,
    up_p,
    down_p,
    act_ref,
    slope_ref,
    back_ref,
    scale_ref,
    spread_ref,
    perm_ref,
    wrecv,
    unit,
    recv,
    work,
    sums_ref,
    mid_ref,
    slots,
    a_sem,
    e_sem,
    z_sem,
    r_sem,
    ax_sem,
    ay_sem,
    by_sem,
    bx_sem,
    f_sem,
    s_sem,
    t_sem,
    o_sem,
    l_sem,
):
    z, y_lo, y_hi, x, core = place()
    y = y_hi * NYL + y_lo
    c = x * 2 + core
    weights = (up_w, down_w)
    parts = (up_p, down_p)

    def remote(src, dst, sems, to):
        return pltpu.make_async_remote_copy(
            src_ref=src,
            dst_ref=dst,
            send_sem=sems.at[0],
            recv_sem=sems.at[1],
            device_id=to,
            device_id_type=MESH,
        )

    started = []

    def start(src, dst, sems, to):
        copy = remote(src, dst, sems, to)
        copy.start()
        started.append(copy)
        return copy

    x_right, x_left, x_far = (x + 1) % NX, (x + 3) % NX, (x + 2) % NX
    to_x = (device(z, y, x_right, core), device(z, y, x_left, core))
    to_y = (device(z, (y + 1) % NY, x, core), device(z, (y + 7) % NY, x, core))
    to_z = (device((z + 1) % NZ, y, x, core), device((z + 11) % NZ, y, x, core))
    to_core = device(z, y, x, 1 - core)
    all_y = [device(z, (y + s) % NY, x, core) for s in range(1, NY)]
    all_c = [device(z, y, ((c + s) % 8) // 2, (c + s) % 2) for s in range(1, 8)]

    for to in all_y + all_c:
        signal(to)
    for to in to_z:
        signal(to)
    for j in (1, 2):
        signal(device((z + 2 * NZ - x - 4 * j) % NZ, y, x, core))
    signal(device((z + NZ - jnp.where(x == 0, 6, x)) % NZ, y, x, core))
    pl.semaphore_wait(pltpu.get_barrier_semaphore(), 19)

    half_cols = pl.ds(aligned(y_hi * HALF, 128), HALF)

    def trade_columns(level):
        copies = []
        for step in (1, 2, 3):
            other = (y_lo + step) % NYL
            copies.append(
                start(
                    wsend_ref.at[level, other],
                    wrecv.at[level, y_lo],
                    e_sem.at[level, step - 1],
                    device(z, y_hi * NYL + other, x, core),
                )
            )
        wrecv[level, y_lo] = wsend_ref[level, y_lo]
        return copies

    trades = [trade_columns(0)]
    b_row = 256 + (x * NYL + y_lo) * 32
    landing = [
        xs.at[core, pl.ds(aligned((y_lo * NX + x) * UNIT, 16), UNIT), half_cols],
        xs.at[core, pl.ds(aligned(b_row, 16), UNIT), half_cols],
        xs.at[core, pl.ds(aligned(b_row + UNIT, 16), UNIT), half_cols],
    ]
    routed = []
    for j in range(3):
        target = (z + x + 4 * j) % NZ
        routed.append(
            remote(
                rows_ref.at[pl.ds(aligned(target * UNIT, 16), UNIT), :],
                landing[j],
                a_sem.at[j],
                device(target, y, x, core),
            )
        )
    own_rows = pltpu.make_async_copy(
        rows_ref.at[pl.ds(aligned(z * UNIT, 16), UNIT), :], landing[0], l_sem
    )
    routed[1].start()
    routed[2].start()

    @pl.when(x == 0)
    def _():
        own_rows.start()

    @pl.when(x != 0)
    def _():
        routed[0].start()

    trades.append(trade_columns(1))

    for level in range(2):
        for zz in range(NZ):
            weights[level][zz * BLOCK + USED : (zz + 1) * BLOCK, :] = jnp.zeros(
                (BLOCK - USED, 512), BF
            )
    sums_ref[...] = jnp.zeros_like(sums_ref)

    def fill_perm(i, carry):
        shape = (16, 704)
        a = lax.broadcasted_iota(jnp.int32, shape, 0) + i * 16
        b = lax.broadcasted_iota(jnp.int32, shape, 1)
        first = sum((a >= 176 * k).astype(jnp.int32) for k in (1, 2, 3))
        rest = a - 176 * first
        second = sum((rest >= 44 * k).astype(jnp.int32) for k in (1, 2, 3))
        perm_ref[pl.ds(aligned(i * 16, 16), 16), :] = jnp.where(
            b == a + 132 * (second - first), 1.0, 0.0
        ).astype(BF)
        return carry

    lax.fori_loop(0, 44, fill_perm, 0)

    zcopies = {}

    def wblock(level, zz, h):
        return weights[level].at[
            pl.ds(aligned(zz * BLOCK, 16), USED), h * 256 : (h + 1) * 256
        ]

    def z_send(level, t, side, h):
        zz = (z + NZ + (-t if side == 0 else t)) % NZ
        dst = wblock(level, zz, h)
        zcopies[level, t, side, h] = start(dst, dst, z_sem.at[level, t, side, h], to_z[side])

    def z_first(level):
        for copy in trades[level]:
            copy.wait_recv()
        pieces = wrecv[level].reshape(4 * USED, 128)
        for m in range(4):
            weights[level][pl.ds(aligned(z * BLOCK, 16), USED), m * 128 : (m + 1) * 128] = jnp.dot(
                perm_ref[m * USED : (m + 1) * USED, :], pieces, preferred_element_type=F32
            ).astype(BF)
        for h in range(2):
            for side in range(2):
                z_send(level, 0, side, h)

    def z_step(level, t):
        for h in range(2):
            for side in range(2):
                zcopies[level, t - 1, side, h].wait_recv()
                if t < 5 or h == side:
                    z_send(level, t, side, h)

    def z_last(level):
        for side in range(2):
            zcopies[level, 5, side, side].wait_recv()

    def a_unit(xx):
        return xs.at[core, pl.ds(aligned((y_lo * NX + xx) * UNIT, 16), UNIT), half_cols]

    def cols_of(yy):
        return pl.ds(aligned((yy // NYL) * HALF, 128), HALF)

    def a_block(yy):
        return xs.at[core, pl.ds(aligned((yy % NYL) * 64, 16), 64), cols_of(yy)]

    def b_chunk(xx, yy):
        return xs.at[
            core, pl.ds(aligned(256 + (xx * NYL + yy % NYL) * 32, 16), 32), cols_of(yy)
        ]

    def b_slab(xx):
        return xs.at[core, pl.ds(aligned(256 + xx * 128, 16), 128), :]

    ycopies = {}

    def y_send(block, name, sems, t):
        for side in range(2 if t < 3 else 1):
            yy = (y + NY + (-t if side == 0 else t)) % NY
            ref = block(yy)
            ycopies[name, t, side] = start(ref, ref, sems.at[t, side], to_y[side])

    def y_wait(name, t):
        for side in range(2 if t < 3 else 1):
            ycopies[name, t, side].wait_recv()

    def b_y_send(t):
        y_send(lambda yy: b_chunk(x, yy), "b", by_sem, t)

    def a_y_send(t):
        y_send(a_block, "a", ay_sem, t)

    xcopies = {}
    fcopies = {}
    scopies = []

    def b_x_send(n):
        ref = b_chunk(x, (y + NY + OFFS[n]) % NY)
        for side in range(2):
            xcopies[n, side] = start(ref, ref, bx_sem.at[n, side], to_x[side])

    def b_forward(n):
        side = n % 2
        xcopies[n, side].wait_recv()
        ref = b_chunk((x_left, x_right)[side], (y + NY + OFFS[n]) % NY)
        fcopies[n] = start(ref, ref, f_sem.at[n], to_x[side])

    def core_send(index, ref):
        scopies.append(start(ref, ref, s_sem.at[index], to_core))

    tcopies = {}

    def sums_send(which, stage):
        src = (sums_ref, mid_ref)[stage].at[which]
        mine = (y, c)[stage]
        tcopies[which, stage] = [
            start(src, slots.at[which, stage, mine], t_sem.at[which, stage, s], to)
            for s, to in enumerate((all_y, all_c)[stage])
        ]
        slots[which, stage, mine] = src[...]

    def sums_wait(which, stage):
        for copy in tcopies[which, stage]:
            copy.wait_recv()
        total = slots[which, stage, 0]
        for i in range(1, 8):
            total += slots[which, stage, i]
        return total

    def picked(product, level):
        masked = product.reshape(12, 16, 512) * mask_ref[level][None]
        total = masked[:, :, :128]
        for m in range(1, 4):
            total = total + masked[:, :, m * 128 : (m + 1) * 128]
        return total.reshape(BLOCK, 128)

    def forward(first, last):
        def body(i, carry):
            here = pl.ds(aligned(i * BLOCK, 16), BLOCK)
            pre = picked(jnp.dot(xs[0, here, :], up_w[...], preferred_element_type=F32), 0)
            act_ref[here, :], slope_ref[here, :] = gelu_pair(pre)
            return carry

        lax.fori_loop(first, last, body, 0)

    def backward(first, last):
        def body(i, carry):
            here = pl.ds(aligned(i * BLOCK, 16), BLOCK)
            back_ref[here, :] = picked(
                jnp.dot(xs[1, here, :], down_w[...], preferred_element_type=F32), 1
            )
            return carry

        lax.fori_loop(first, last, body, 0)

    def row_sums(which, left, right):
        for k in range(6):
            here = slice(k * 128, (k + 1) * 128)
            sums_ref[which, k : k + 1, :] = jnp.sum(
                (left[here, :] * right[here, :]).T, axis=0, keepdims=True
            )

    def column(row):
        return jnp.broadcast_to(row, (128, 128)).T

    def store_spread(k, values):
        here = slice(k * 128, (k + 1) * 128)
        path = (lax.broadcasted_iota(jnp.int32, (128, 128), 0) // 4) % 4
        for i in range(4):
            spread_ref[here, i * 128 : (i + 1) * 128] = jnp.where(path == i, values, 0.0).astype(BF)

    def make_hidden(total):
        scale_row = jnp.sqrt(total / FF + hidden_epsilon)
        for k in range(6):
            here = slice(k * 128, (k + 1) * 128)
            scale = column(scale_row[k : k + 1, :])
            scale_ref[here, :] = scale
            hidden = act_ref[here, :] / scale
            act_ref[here, :] = hidden
            store_spread(k, hidden)

    def make_dpre(total):
        mix_row = total / FF
        for k in range(6):
            here = slice(k * 128, (k + 1) * 128)
            mixing = column(mix_row[k : k + 1, :])
            hidden = act_ref[here, :]
            store_spread(
                k,
                (back_ref[here, :] - hidden * mixing) / scale_ref[here, :] * slope_ref[here, :],
            )

    def turn(which, first, last):
        def body(i, carry):
            here = pl.ds(aligned(i * 128, 128), 128)
            xt[which, here, :] = xs[which, :, here].T
            return carry

        lax.fori_loop(first, last, body, 0)

    def gradient(which, first, last):
        def body(i, carry):
            here = pl.ds(aligned(i * 384, 128), 384)
            grads[here, :] = jnp.dot(
                xt[which, here, :], spread_ref[...], preferred_element_type=F32
            )
            return carry

        lax.fori_loop(first, last, body, 0)

    q_first = ((z + 6) % NZ) // 2

    def deltas(level, offset):
        base = ((q_first + 6 + offset) % 6) * 384
        choice = [[pick_ref[level, i * 4 + m] for m in range(4)] for i in range(4)]

        def body(i, carry):
            here = pl.ds(aligned(base + i * 32, 32), 32)
            modules = [
                weights[level][here, m * 128 : (m + 1) * 128].astype(F32) for m in range(4)
            ]
            totals = [None] * 4
            for p in range(4):
                gradient_p = grads[here, p * 128 : (p + 1) * 128]
                weight_p = choice[p][0] * modules[0]
                for m in range(1, 4):
                    weight_p = weight_p + choice[p][m] * modules[m]
                update = gradient_p / (jnp.abs(gradient_p) + adam_epsilon) + decay_rate * weight_p
                delta = (-inner_rate * update).astype(BF).astype(F32)
                for m in range(4):
                    term = choice[p][m] * delta
                    totals[m] = term if p == 0 else totals[m] + term
            for m in range(4):
                parts[level][here, m * 128 : (m + 1) * 128] = totals[m].astype(BF)
            return carry

        lax.fori_loop(0, 12, body, 0)

    rcopies = {}

    def pblock(level, zz, h):
        return parts[level].at[
            pl.ds(aligned(zz * BLOCK, 16), USED), h * 256 : (h + 1) * 256
        ]

    def ring(level, t):
        for h in range(2):
            for side in range(2):
                if t == 0 and h != side:
                    continue
                zz = (z + (6 - t if side == 0 else NZ - 6 + t)) % NZ
                src = pblock(level, zz, h)
                if (level, t - 1, side, h) in rcopies:
                    rcopies[level, t - 1, side, h].wait_recv()
                    held = recv.at[level, side, t - 1, h]
                    held[...] = (held[...].astype(F32) + src[...].astype(F32)).astype(BF)
                    src = held
                rcopies[level, t, side, h] = start(
                    src, recv.at[level, side, t, h], r_sem.at[level, t, side, h], to_z[side]
                )

    ocopies = []

    def finish(level):
        pieces = []
        for h in range(2):
            for side in range(2):
                rcopies[level, 5, side, h].wait_recv()
            total = (
                pblock(level, z, h)[...].astype(F32)
                + recv[level, 0, 5, h].astype(F32)
                + recv[level, 1, 5, h].astype(F32)
            ).astype(BF)
            pieces += [total[:, :128], total[:, 128:]]
        work[level] = (
            jnp.dot(perm_ref[...], jnp.concatenate(pieces, axis=0), preferred_element_type=F32)
            .astype(BF)
            .reshape(4, USED, 128)
        )
        for step in (1, 2, 3):
            other = (y_lo + step) % NYL
            ocopies.append(
                start(
                    work.at[level, other],
                    out_ref.at[level, y_lo],
                    o_sem.at[level, step - 1],
                    device(z, y_hi * NYL + other, x, core),
                )
            )
        out_ref[level, y_lo] = work[level, y_lo]

    z_first(0)
    routed[1].wait_recv()
    routed[2].wait_recv()
    b_y_send(0)
    b_x_send(0)

    @pl.when(x == 0)
    def _():
        own_rows.wait()

    @pl.when(x != 0)
    def _():
        routed[0].wait_recv()

    own = a_unit(x)
    a_right = start(own, own, ax_sem.at[0], to_x[0])
    a_left = start(own, own, ax_sem.at[1], to_x[1])
    a_right.wait_recv()
    passed = a_unit(x_left)
    a_far = start(passed, passed, ax_sem.at[2], to_x[0])
    y_wait("b", 0)
    b_y_send(1)
    b_x_send(1)
    b_x_send(2)
    a_left.wait_recv()
    a_far.wait_recv()
    a_y_send(0)
    z_first(1)
    z_step(0, 1)
    y_wait("b", 1)
    b_y_send(2)
    b_x_send(3)
    b_x_send(4)
    y_wait("a", 0)
    a_y_send(1)
    y_wait("b", 2)
    b_y_send(3)
    b_x_send(5)
    b_x_send(6)
    z_step(0, 2)
    y_wait("b", 3)
    b_x_send(7)
    core_send(0, b_slab(x))
    y_wait("a", 1)
    a_y_send(2)
    b_forward(0)
    b_forward(1)
    z_step(0, 3)
    y_wait("a", 2)
    a_y_send(3)
    b_forward(2)
    b_forward(3)
    z_step(0, 4)
    b_forward(4)
    b_forward(5)
    y_wait("a", 3)
    core_send(1, xs.at[core, pl.ds(0, 256), :])
    z_step(1, 1)
    b_forward(6)
    b_forward(7)
    z_step(0, 5)
    for n in range(8):
        xcopies[n, 1 - n % 2].wait_recv()
    core_send(2, b_slab(x_left))
    core_send(3, b_slab(x_right))
    for n in range(8):
        fcopies[n].wait_recv()
    core_send(4, b_slab(x_far))
    z_step(1, 2)
    z_last(0)
    for copy in scopies:
        copy.wait_recv()

    forward(0, 2)
    forward(2, 4)
    row_sums(0, act_ref, act_ref)
    sums_send(0, 0)
    z_step(1, 3)
    turn(1, 0, 9)
    mid_ref[0] = sums_wait(0, 0)
    sums_send(0, 1)
    turn(1, 9, 18)
    z_step(1, 4)
    squares = sums_wait(0, 1)
    make_hidden(squares)
    gradient(1, 0, 3)
    z_step(1, 5)
    gradient(1, 3, 6)
    z_last(1)

    deltas(1, 0)
    ring(1, 0)
    deltas(1, -1)
    deltas(1, 1)
    backward(0, 2)
    ring(1, 1)
    deltas(1, -2)
    deltas(1, 2)
    backward(2, 4)
    row_sums(1, back_ref, act_ref)
    sums_send(1, 0)
    ring(1, 2)
    deltas(1, 3)
    turn(0, 0, 9)
    mid_ref[1] = sums_wait(1, 0)
    sums_send(1, 1)
    ring(1, 3)
    turn(0, 9, 18)
    products = sums_wait(1, 1)
    make_dpre(products)
    gradient(0, 0, 3)
    ring(1, 4)
    gradient(0, 3, 6)
    deltas(0, 0)
    ring(1, 5)
    ring(0, 0)
    deltas(0, -1)
    deltas(0, 1)
    ring(0, 1)
    finish(1)
    deltas(0, -2)
    deltas(0, 2)
    ring(0, 2)
    deltas(0, 3)
    for t in (3, 4, 5):
        ring(0, t)
    finish(0)

    for copy in ocopies:
        copy.wait_recv()
    for copy in started:
        copy.wait_send()
    routed[1].wait_send()
    routed[2].wait_send()

    @pl.when(x != 0)
    def _():
        routed[0].wait_send()


VMEM = pl.BlockSpec(memory_space=pltpu.VMEM)
SMEM = pl.BlockSpec(memory_space=pltpu.SMEM)
DMA = pltpu.SemaphoreType.DMA


def fused(rows, weights, masks, picks):
    return pl.pallas_call(
        fused_kernel,
        out_shape=jax.ShapeDtypeStruct((2, 4, USED, 128), BF),
        in_specs=[VMEM, VMEM, VMEM, SMEM],
        out_specs=VMEM,
        scratch_shapes=[
            pltpu.VMEM((2, PLANE, WIDE), BF),
            pltpu.VMEM((2, WIDE, PLANE), BF),
            pltpu.VMEM((WIDE, 512), BF),
            pltpu.VMEM((WIDE, 512), BF),
            pltpu.VMEM((WIDE, 512), F32),
            pltpu.VMEM((WIDE, 512), BF),
            pltpu.VMEM((WIDE, 512), BF),
            pltpu.VMEM((PLANE, 128), F32),
            pltpu.VMEM((PLANE, 128), F32),
            pltpu.VMEM((PLANE, 128), F32),
            pltpu.VMEM((PLANE, 128), F32),
            pltpu.VMEM((PLANE, 512), BF),
            pltpu.VMEM((704, 704), BF),
            pltpu.VMEM((2, 4, USED, 128), BF),
            pltpu.VMEM((2, USED, 512), BF),
            pltpu.VMEM((2, 2, 6, 2, USED, 256), BF),
            pltpu.VMEM((2, 4, USED, 128), BF),
            pltpu.VMEM((2, 8, 128), F32),
            pltpu.VMEM((2, 8, 128), F32),
            pltpu.VMEM((2, 2, 8, 8, 128), F32),
            DMA((3, 2)),
            DMA((2, 3, 2)),
            DMA((2, 6, 2, 2, 2)),
            DMA((2, 6, 2, 2, 2)),
            DMA((3, 2)),
            DMA((4, 2, 2)),
            DMA((4, 2, 2)),
            DMA((8, 2, 2)),
            DMA((8, 2)),
            DMA((5, 2)),
            DMA((2, 2, 7, 2)),
            DMA((2, 3, 2)),
            DMA,
        ],
        compiler_params=pltpu.CompilerParams(
            collective_id=0, has_side_effects=True, vmem_limit_bytes=56 * 1024 * 1024
        ),
        name="fused",
    )(rows, weights, masks, picks)


def on_device(
    tokens,
    out_grad,
    doc_lengths,
    doc_paths,
    membership,
    up_master,
    down_master,
    up_moment,
    down_moment,
):
    path_count = lax.axis_size("path")
    row_count, width = tokens.shape
    module_count, owner_rows, owner_columns = up_master.shape
    capacity = row_count // path_count
    z, y_lo, y_hi, x, core = place()

    placing = placing_matrix(doc_lengths[0], doc_paths[0], row_count, path_count, capacity)
    rows_float = tokens.astype(F32)
    normed = (
        rows_float
        * lax.rsqrt(jnp.mean(rows_float * rows_float, axis=1, keepdims=True) + norm_epsilon)
    ).astype(BF)
    chosen = jnp.where(core == 0, normed, out_grad)
    half = jnp.where(y_hi == 0, chosen[:, : width // 2], chosen[:, width // 2 :])
    rows = jnp.dot(placing, half, preferred_element_type=F32).astype(BF)
    rows = jnp.concatenate(
        [
            jnp.pad(rows[:, k * USED : (k + 1) * USED], ((0, 0), (0, BLOCK - USED)))
            for k in range(NZ // 2)
        ],
        axis=1,
    )

    def blocks(master):
        flat = master.astype(BF).reshape(module_count * owner_rows, NYL, 128)
        return flat.transpose(1, 0, 2)

    weights_out = jnp.stack([blocks(up_master), blocks(down_master)])

    members = lax.dynamic_slice_in_dim(membership, z * NYL, NYL, 0)
    module_ids = jnp.arange(module_count, dtype=jnp.int32)
    picks = (members.T[:, :, None] == module_ids).astype(F32)
    masks = jnp.repeat(jnp.repeat(picks, capacity, axis=1), 128, axis=2)

    summed = fused(rows, weights_out, masks, picks.reshape(2, NYL * module_count))

    def update(master, moment, level):
        counts = jnp.sum((membership[:, level][None, :] == module_ids[:, None]).astype(F32), axis=1)
        total = (
            summed[level]
            .reshape(NYL, module_count, owner_rows, 128)
            .transpose(1, 2, 0, 3)
            .reshape(module_count, owner_rows, owner_columns)
        )
        return outer_update(master, moment, total.astype(F32), counts)

    new_up, new_up_moment = update(up_master, up_moment, 0)
    new_down, new_down_moment = update(down_master, down_moment, 1)
    return (new_up, new_down, new_up_moment, new_down_moment)


def solution(mesh):
    split = P(None, "path", "shard")
    rows = P("path", None)
    return jax.shard_map(
        on_device,
        mesh=mesh,
        in_specs=(rows, rows, rows, rows, P(), split, split, split, split),
        out_specs=(split, split, split, split),
        check_vma=False,
    )
```

```python
import functools

import jax
import jax.numpy as jnp
from jax import lax
from jax.experimental import pallas as pl
from jax.experimental.pallas import tpu as pltpu
from jax.sharding import PartitionSpec as P

MESH = pl.DeviceIdType.MESH
BF = jnp.bfloat16
F32 = jnp.float32

FF = 8192
NZ = 12
NYL = 4
NY = 8
NX = 4
UNIT = 16
HALF = 1152
WIDE = 2304
BLOCK = 192
USED = 176
PLANE = 768
PART = (96, 80)
OFFS = (0, -1, 1, -2, 2, -3, 3, -4)

norm_epsilon = 1e-06
hidden_epsilon = 1e-05
adam_epsilon = 0.001
inner_rate = 0.05
decay_rate = 0.1
outer_rate = 0.7
momentum_coef = 0.9
gelu_coef = 0.7978845608
cubic_coef = 0.044715


def gelu_pair(values):
    inner = gelu_coef * (values + cubic_coef * values * values * values)
    tangent = jnp.tanh(inner)
    activated = 0.5 * values * (1.0 + tangent)
    slopes = 0.5 * (1.0 + tangent) + 0.5 * values * (1.0 - tangent * tangent) * gelu_coef * (
        1.0 + 3.0 * cubic_coef * values * values
    )
    return (activated, slopes)


def row_slots(lengths, targets, row_count, path_count, capacity):
    ends = jnp.cumsum(lengths)
    row_ids = jnp.arange(row_count, dtype=jnp.int32)
    doc_of_row = jnp.sum((row_ids[:, None] >= ends[None, :]).astype(jnp.int32), axis=1)
    doc_hit = doc_of_row[:, None] == jnp.arange(lengths.shape[0], dtype=jnp.int32)[None, :]
    row_path = jnp.sum(jnp.where(doc_hit, targets[None, :], 0), axis=1)
    path_hit = (row_path[:, None] == jnp.arange(path_count, dtype=jnp.int32)[None, :]).astype(
        jnp.int32
    )
    ranks = jnp.sum((jnp.cumsum(path_hit, axis=0) - 1) * path_hit, axis=1)
    return jnp.where(ranks < capacity, row_path * capacity + ranks, -1)


def outer_update(master, moment, summed, counts):
    pseudo = -summed / jnp.maximum(counts, 1.0)[:, None, None]
    buffer = momentum_coef * moment.astype(jnp.float32) + pseudo
    return (master - outer_rate * (pseudo + momentum_coef * buffer), buffer.astype(jnp.bfloat16))


def place():
    path = lax.axis_index("path")
    shard = lax.axis_index("shard")
    return path // NYL, path % NYL, shard // 8, (shard // 2) % NX, shard % 2


def device(z, y, x, core):
    return (z * NYL + y % NYL, ((y // NYL) * NX + x) * 2 + core)


def aligned(value, multiple):
    return pl.multiple_of(value, multiple)


def signal(to):
    pl.semaphore_signal(
        pltpu.get_barrier_semaphore(), inc=1, device_id=to, device_id_type=MESH
    )


def fused_kernel(
    tokens,
    out_grad,
    slots_ref,
    up_master,
    down_master,
    member_ref,
    up_sums,
    down_sums,
    mask_ref,
    total_ref,
    padded,
    chosen_ref,
    blocks_ref,
    wsend_ref,
    landed,
    back_perm,
    xs,
    xt,
    up_w,
    down_w,
    grads,
    up_p,
    down_p,
    act_ref,
    slope_ref,
    back_ref,
    scale_ref,
    spread_ref,
    perm_ref,
    wrecv,
    recv,
    work,
    sums_ref,
    mid_ref,
    slots,
    a_sem,
    e_sem,
    z_sem,
    r_sem,
    ax_sem,
    ay_sem,
    by_sem,
    bx_sem,
    f_sem,
    s_sem,
    t_sem,
    o_sem,
    l_sem,
):
    z, y_lo, y_hi, x, core = place()
    y = y_hi * NYL + y_lo
    c = x * 2 + core
    weights = (up_w, down_w)
    masters = (up_master, down_master)
    outputs = (up_sums, down_sums)
    parts = (up_p, down_p)

    def remote(src, dst, sems, to):
        return pltpu.make_async_remote_copy(
            src_ref=src,
            dst_ref=dst,
            send_sem=sems.at[0],
            recv_sem=sems.at[1],
            device_id=to,
            device_id_type=MESH,
        )

    started = []

    def start(src, dst, sems, to):
        copy = remote(src, dst, sems, to)
        copy.start()
        started.append(copy)
        return copy

    x_right, x_left, x_far = (x + 1) % NX, (x + 3) % NX, (x + 2) % NX
    to_x = (device(z, y, x_right, core), device(z, y, x_left, core))
    to_y = (device(z, (y + 1) % NY, x, core), device(z, (y + 7) % NY, x, core))
    to_z = (device((z + 1) % NZ, y, x, core), device((z + 11) % NZ, y, x, core))
    to_core = device(z, y, x, 1 - core)
    all_y = [device(z, (y + s) % NY, x, core) for s in range(1, NY)]
    all_c = [device(z, y, ((c + s) % 8) // 2, (c + s) % 2) for s in range(1, 8)]

    for to in all_y + all_c:
        signal(to)
    for to in to_z:
        signal(to)
    hops = [
        jnp.where(x == 0, a, jnp.where(x == 1, b, jnp.where(x == 2, c_, d)))
        for a, b, c_, d in ((0, 1, 2, 6), (5, 4, 3, 9), (7, 8, 11, 10))
    ]
    signal(device((z + NZ - jnp.where(x == 0, 6, hops[0])) % NZ, y, x, core))
    for j in (1, 2):
        signal(device((z + NZ - hops[j]) % NZ, y, x, core))
    for level in range(2):
        for other in range(4):
            for m in range(4):
                wsend_ref[level, other, m * 48 + 32 : m * 48 + 48, :] = jnp.zeros((16, 128), BF)
    for level in range(2):
        for m in range(4):
            values = masters[level][:, m, :].astype(BF)
            for other in range(4):
                wsend_ref[level, other, m * 48 : m * 48 + 44, :] = values[
                    :, other * 128 : (other + 1) * 128
                ]
    rows_float = tokens[...].astype(F32)
    normed = (
        rows_float
        * lax.rsqrt(jnp.mean(rows_float * rows_float, axis=1, keepdims=True) + norm_epsilon)
    ).astype(BF)
    chosen_ref[...] = jnp.where(core == 0, normed, out_grad[...])
    blocks_ref[...] = jnp.zeros_like(blocks_ref)
    for n in range(NZ // 2):
        low = chosen_ref[:, n * USED : (n + 1) * USED]
        high = chosen_ref[:, (n + 6) * USED : (n + 7) * USED]
        blocks_ref[:, n * BLOCK : n * BLOCK + USED] = jnp.where(y_hi == 0, low, high)
    placing = (lax.broadcasted_iota(jnp.int32, (192, 192), 0) == slots_ref[...]).astype(F32)
    padded[...] = jnp.dot(
        placing.astype(BF), blocks_ref[...], preferred_element_type=F32
    ).astype(BF)
    pl.semaphore_wait(pltpu.get_barrier_semaphore(), 19)

    half_cols = pl.ds(aligned(y_hi * HALF, 128), HALF)

    def trade_columns(level):
        copies = []
        for step in (1, 2, 3):
            other = (y_lo + step) % NYL
            copies.append(
                start(
                    wsend_ref.at[level, other],
                    wrecv.at[level, y_lo],
                    e_sem.at[level, step - 1],
                    device(z, y_hi * NYL + other, x, core),
                )
            )
        wrecv[level, y_lo] = wsend_ref[level, y_lo]
        return copies

    trades = [trade_columns(0)]
    b_row = 256 + (x * NYL + y_lo) * 32
    landing = [
        xs.at[core, pl.ds(aligned((y_lo * NX + x) * UNIT, 16), UNIT), half_cols],
        xs.at[core, pl.ds(aligned(b_row, 16), UNIT), half_cols],
        xs.at[core, pl.ds(aligned(b_row + UNIT, 16), UNIT), half_cols],
    ]
    routed = []
    for j in range(3):
        target = (z + hops[j]) % NZ
        routed.append(
            remote(
                padded.at[pl.ds(aligned(target * UNIT, 16), UNIT), :],
                landing[j],
                a_sem.at[j],
                device(target, y, x, core),
            )
        )
    own_rows = pltpu.make_async_copy(
        padded.at[pl.ds(aligned(z * UNIT, 16), UNIT), :], landing[0], l_sem
    )
    routed[1].start()
    routed[2].start()

    @pl.when(x == 0)
    def _():
        own_rows.start()

    @pl.when(x != 0)
    def _():
        routed[0].start()

    for level in range(2):
        for zz in range(NZ):
            weights[level][zz * BLOCK + USED : (zz + 1) * BLOCK, :] = jnp.zeros(
                (BLOCK - USED, 512), BF
            )
    sums_ref[...] = jnp.zeros_like(sums_ref)
    choice = [
        [
            [jnp.where(member_ref[level, z * NYL + i] == m, 1.0, 0.0) for m in range(4)]
            for i in range(4)
        ]
        for level in range(2)
    ]
    path_of_row = lax.broadcasted_iota(jnp.int32, (16, 128), 0) // 4
    for level in range(2):
        for m in range(4):
            mask_ref[level, :, m * 128 : (m + 1) * 128] = sum(
                jnp.where(path_of_row == i, choice[level][i][m], 0.0) for i in range(4)
            )

    def fill_perm(i, carry):
        here = pl.ds(aligned(i * 16, 16), 16)
        a = lax.broadcasted_iota(jnp.int32, (16, 1), 0) + i * 16
        b = lax.broadcasted_iota(jnp.int32, (16, 768), 1)
        first = sum((a >= 176 * n).astype(jnp.int32) for n in (1, 2, 3))
        rest = a - 176 * first
        second = sum((rest >= 44 * n).astype(jnp.int32) for n in (1, 2, 3))
        to_b = second * 192 + first * 48 + rest - 44 * second
        perm_ref[here, :] = jnp.where(b == to_b, 1.0, 0.0).astype(BF)
        return carry

    def fill_back(i, carry):
        here = pl.ds(aligned(i * 16, 16), 16)
        b = lax.broadcasted_iota(jnp.int32, (16, 1), 0) + i * 16
        a = lax.broadcasted_iota(jnp.int32, (16, 704), 1)
        first = sum((b >= 192 * n).astype(jnp.int32) for n in (1, 2, 3))
        rest = b - 192 * first
        second = sum((rest >= 48 * n).astype(jnp.int32) for n in (1, 2, 3))
        row = rest - 48 * second
        to_a = jnp.where(row < 44, second * 176 + first * 44 + row, -1)
        back_perm[here, :] = jnp.where(a == to_a, 1.0, 0.0).astype(BF)
        return carry

    def constants():
        lax.fori_loop(0, 48, fill_back, 0)

    lax.fori_loop(0, 44, fill_perm, 0)

    zcopies = {}

    def wblock(level, zz, h):
        return weights[level].at[
            pl.ds(aligned(zz * BLOCK, 16), USED), h * 256 : (h + 1) * 256
        ]

    def z_send(level, t, side, h):
        zz = (z + NZ + (-t if side == 0 else t)) % NZ
        dst = wblock(level, zz, h)
        zcopies[level, t, side, h] = start(dst, dst, z_sem.at[level, t, side, h], to_z[side])

    def z_first(level):
        for copy in trades[level]:
            copy.wait_recv()
        pieces = wrecv[level].reshape(4 * BLOCK, 128)
        for m in range(4):
            weights[level][pl.ds(aligned(z * BLOCK, 16), USED), m * 128 : (m + 1) * 128] = jnp.dot(
                perm_ref[m * USED : (m + 1) * USED, :], pieces, preferred_element_type=F32
            ).astype(BF)
        for h in range(2):
            for side in range(2):
                z_send(level, 0, side, h)

    def z_got(level, t, side, h):
        zcopies[level, t, side, h].wait_recv()
        if t < 4 or (t == 4 and h == side):
            z_send(level, t + 1, side, h)

    def a_unit(xx):
        return a_part(xx, y)

    def cols_of(yy):
        return pl.ds(aligned((yy // NYL) * HALF, 128), HALF)

    def a_part(xx, yy):
        return xs.at[
            core, pl.ds(aligned(((yy % NYL) * NX + xx) * UNIT, 16), UNIT), cols_of(yy)
        ]

    def b_chunk(xx, yy):
        return xs.at[
            core, pl.ds(aligned(256 + (xx * NYL + yy % NYL) * 32, 16), 32), cols_of(yy)
        ]

    def b_slab(xx):
        return xs.at[core, pl.ds(aligned(256 + xx * 128, 16), 128), :]

    ycopies = {}

    def y_send(name, block, sems, t, side):
        ref = block((y + NY + (-t if side == 0 else t)) % NY)
        ycopies[name, t, side] = start(ref, ref, sems.at[t, side], to_y[side])

    def b_y_send(t, side):
        y_send("b", lambda yy: b_chunk(x, yy), by_sem, t, side)

    def a_y_send(k, t, side):
        y_send(k, lambda yy: a_part(lanes_a[k], yy), ay_sem.at[k], t, side)

    def onward(t, side):
        return t < 3 and (side == 0 or t < 2)

    lanes_a = (x, x_left, x_right, x_far)
    xcopies = {}
    fcopies = {}
    acopies = {}
    scopies = []

    def b_x_send(n):
        ref = b_chunk(x, (y + NY + OFFS[n]) % NY)
        for side in range(2):
            xcopies[n, side] = start(ref, ref, bx_sem.at[n, side], to_x[side])

    def core_send(index):
        ref = xs.at[core, pl.ds(0, 256), :] if index == 1 else b_slab((x, x, x_left, x_right, x_far)[index])
        scopies.append(start(ref, ref, s_sem.at[len(scopies)], to_core))

    def rows_got():
        routed[1].wait_recv()
        routed[2].wait_recv()
        b_y_send(0, 0)
        b_y_send(0, 1)

        @pl.when(x == 0)
        def _():
            own_rows.wait()

        @pl.when(x != 0)
        def _():
            routed[0].wait_recv()

        own = a_unit(x)
        for side in range(2):
            acopies[side] = start(own, own, ax_sem.at[side], to_x[side])
        a_y_send(0, 0, 0)
        a_y_send(0, 0, 1)
        b_x_send(0)

    def a_x_got(i):
        acopies[i].wait_recv()
        if i == 0:
            passed = a_unit(x_left)
            acopies[2] = start(passed, passed, ax_sem.at[2], to_x[0])
        a_y_send(i + 1, 0, 0)
        a_y_send(i + 1, 0, 1)

    def b_y_got(t, side):
        ycopies["b", t, side].wait_recv()
        if onward(t, side):
            b_y_send(t + 1, side)
        b_x_send(2 * t + 1 + side)

    def a_y_got(k, t, side):
        ycopies[k, t, side].wait_recv()
        if onward(t, side):
            a_y_send(k, t + 1, side)

    def b_x_got(n, side):
        xcopies[n, side].wait_recv()
        if n % 2 == side:
            ref = b_chunk((x_left, x_right)[side], (y + NY + OFFS[n]) % NY)
            fcopies[n] = start(ref, ref, f_sem.at[n], to_x[side])

    def f_got(n):
        fcopies[n].wait_recv()

    tcopies = {}

    def sums_send(which, stage):
        src = (sums_ref, mid_ref)[stage].at[which]
        mine = (y, c)[stage]
        tcopies[which, stage] = [
            start(src, slots.at[which, stage, mine], t_sem.at[which, stage, s], to)
            for s, to in enumerate((all_y, all_c)[stage])
        ]
        slots[which, stage, mine] = src[...]

    def sums_wait(which, stage):
        for copy in tcopies[which, stage]:
            copy.wait_recv()
        total = slots[which, stage, 0]
        for i in range(1, 8):
            total += slots[which, stage, i]
        return total

    def picked(product, level):
        masked = product.reshape(12, 16, 512) * mask_ref[level][None]
        total = masked[:, :, :128]
        for m in range(1, 4):
            total = total + masked[:, :, m * 128 : (m + 1) * 128]
        return total.reshape(BLOCK, 128)

    def forward(first, last):
        def body(i, carry):
            here = pl.ds(aligned(i * BLOCK, 16), BLOCK)
            pre = picked(jnp.dot(xs[0, here, :], up_w[...], preferred_element_type=F32), 0)
            act_ref[here, :], slope_ref[here, :] = gelu_pair(pre)
            return carry

        lax.fori_loop(first, last, body, 0)

    def backward(first, last):
        def body(i, carry):
            here = pl.ds(aligned(i * BLOCK, 16), BLOCK)
            back_ref[here, :] = picked(
                jnp.dot(xs[1, here, :], down_w[...], preferred_element_type=F32), 1
            )
            return carry

        lax.fori_loop(first, last, body, 0)

    def row_sums(which, left, right):
        for k in range(6):
            here = slice(k * 128, (k + 1) * 128)
            sums_ref[which, k : k + 1, :] = jnp.sum(
                (left[here, :] * right[here, :]).T, axis=0, keepdims=True
            )

    def column(row):
        return jnp.broadcast_to(row, (128, 128)).T

    def store_spread(k, values):
        here = slice(k * 128, (k + 1) * 128)
        path = (lax.broadcasted_iota(jnp.int32, (128, 128), 0) // 4) % 4
        for i in range(4):
            spread_ref[here, i * 128 : (i + 1) * 128] = jnp.where(path == i, values, 0.0).astype(BF)

    def make_hidden(total):
        scale_row = jnp.sqrt(total / FF + hidden_epsilon)
        for k in range(6):
            here = slice(k * 128, (k + 1) * 128)
            scale = column(scale_row[k : k + 1, :])
            scale_ref[here, :] = scale
            hidden = act_ref[here, :] / scale
            act_ref[here, :] = hidden
            store_spread(k, hidden)

    def make_dpre(total):
        mix_row = total / FF
        for k in range(6):
            here = slice(k * 128, (k + 1) * 128)
            mixing = column(mix_row[k : k + 1, :])
            hidden = act_ref[here, :]
            store_spread(
                k,
                (back_ref[here, :] - hidden * mixing) / scale_ref[here, :] * slope_ref[here, :],
            )

    def turn(which, first, last):
        def body(i, carry):
            here = pl.ds(aligned(i * 128, 128), 128)
            xt[which, here, :] = xs[which, :, here].T
            return carry

        lax.fori_loop(first, last, body, 0)

    def gradient(which, first, last):
        def body(i, carry):
            here = pl.ds(aligned(i * 384, 128), 384)
            grads[here, :] = jnp.dot(
                xt[which, here, :], spread_ref[...], preferred_element_type=F32
            )
            return carry

        lax.fori_loop(first, last, body, 0)

    q_first = ((z + 6) % NZ) // 2

    def deltas(level, offset):
        base = ((q_first + 6 + offset) % 6) * 384
        chosen = choice[level]

        def body(i, carry):
            here = pl.ds(aligned(base + i * 32, 32), 32)
            modules = [
                weights[level][here, m * 128 : (m + 1) * 128].astype(F32) for m in range(4)
            ]
            totals = [None] * 4
            for p in range(4):
                gradient_p = grads[here, p * 128 : (p + 1) * 128]
                weight_p = chosen[p][0] * modules[0]
                for m in range(1, 4):
                    weight_p = weight_p + chosen[p][m] * modules[m]
                size = jnp.abs(gradient_p) + adam_epsilon
                inverse = pl.reciprocal(size, approx=True)
                inverse = inverse * (2.0 - size * inverse)
                update = gradient_p * inverse + decay_rate * weight_p
                delta = (-inner_rate * update).astype(BF).astype(F32)
                for m in range(4):
                    term = chosen[p][m] * delta
                    totals[m] = term if p == 0 else totals[m] + term
            for m in range(4):
                parts[level][here, m * 128 : (m + 1) * 128] = totals[m].astype(BF)
            return carry

        lax.fori_loop(0, 12, body, 0)

    rcopies = {}

    def pblock(level, zz, h):
        return parts[level].at[
            pl.ds(aligned(zz * BLOCK + 96 * h, 16), PART[h]), :
        ]

    def held_part(level, side, t, h):
        return recv.at[level, side, t, 96 * h : 96 * h + PART[h], :]

    def ring_part(level, t, side, h):
        zz = (z + (6 - t if side == 0 else NZ - 6 + t)) % NZ
        src = pblock(level, zz, h)
        if (level, t - 1, side, h) in rcopies:
            rcopies[level, t - 1, side, h].wait_recv()
            held = held_part(level, side, t - 1, h)
            held[...] = (held[...].astype(F32) + src[...].astype(F32)).astype(BF)
            src = held
        rcopies[level, t, side, h] = start(
            src, held_part(level, side, t, h), r_sem.at[level, t, side, h], to_z[side]
        )

    ocopies = {}

    def finish(level):
        totals = []
        for h in range(2):
            for side in range(2):
                rcopies[level, 5, side, h].wait_recv()
            totals.append(
                pblock(level, z, h)[...].astype(F32)
                + held_part(level, 0, 5, h)[...].astype(F32)
                + held_part(level, 1, 5, h)[...].astype(F32)
            )
        total = jnp.concatenate(totals, axis=0).astype(BF)
        pieces = [total[:, m * 128 : (m + 1) * 128] for m in range(4)]
        work[level] = (
            jnp.dot(back_perm[...], jnp.concatenate(pieces, axis=0), preferred_element_type=F32)
            .astype(BF)
            .reshape(4, BLOCK, 128)
        )
        for step in (1, 2, 3):
            other = (y_lo + step) % NYL
            ocopies[level, step] = start(
                work.at[level, other],
                landed.at[level, y_lo],
                o_sem.at[level, step - 1],
                device(z, y_hi * NYL + other, x, core),
            )
        landed[level, y_lo] = work[level, y_lo]

    def outer(level):
        for step in (1, 2, 3):
            ocopies[level, step].wait_recv()
        for m in range(4):
            total_ref[:, m, :] = jnp.concatenate(
                [landed[level, n, m * 48 : m * 48 + 44, :].astype(F32) for n in range(4)], axis=1
            )
        outputs[level][...] = total_ref[...].astype(BF)

    z_first(0)
    constants()
    rows_got()
    z_got(0, 0, 0, 0)
    z_got(0, 0, 1, 0)
    a_x_got(0)
    a_x_got(1)
    b_y_got(0, 0)
    z_got(0, 0, 0, 1)
    b_y_got(0, 1)
    z_got(0, 0, 1, 1)
    a_y_got(0, 0, 0)
    a_y_got(0, 0, 1)
    b_x_got(0, 0)
    b_x_got(0, 1)
    a_x_got(2)
    a_y_got(1, 0, 0)
    z_got(0, 1, 0, 0)
    a_y_got(1, 0, 1)
    z_got(0, 1, 1, 0)
    a_y_got(2, 0, 0)
    a_y_got(2, 0, 1)
    b_x_got(1, 0)
    b_x_got(1, 1)
    z_got(0, 1, 0, 1)
    b_y_got(1, 0)
    trades.append(trade_columns(1))
    b_y_got(1, 1)
    z_got(0, 1, 1, 1)
    b_x_got(2, 0)
    a_y_got(0, 1, 0)
    b_x_got(2, 1)
    a_y_got(0, 1, 1)
    a_y_got(3, 0, 0)
    a_y_got(3, 0, 1)
    z_got(0, 2, 0, 0)
    f_got(0)
    a_y_got(1, 1, 0)
    a_y_got(1, 1, 1)
    z_got(0, 2, 1, 0)
    f_got(1)
    a_y_got(2, 1, 0)
    a_y_got(2, 1, 1)
    b_x_got(3, 0)
    z_got(0, 2, 0, 1)
    b_x_got(3, 1)
    b_y_got(2, 0)
    z_got(0, 2, 1, 1)
    b_x_got(4, 0)
    b_x_got(4, 1)
    z_got(0, 3, 0, 0)
    f_got(2)
    z_got(0, 3, 1, 0)
    f_got(3)
    z_got(0, 3, 0, 1)
    b_x_got(5, 0)
    b_y_got(2, 1)
    z_first(1)
    z_got(0, 3, 1, 1)
    a_y_got(0, 2, 0)
    a_y_got(0, 2, 1)
    b_x_got(5, 1)
    a_y_got(3, 1, 0)
    f_got(4)
    a_y_got(3, 1, 1)
    z_got(0, 4, 0, 0)
    a_y_got(1, 2, 0)
    a_y_got(1, 2, 1)
    z_got(0, 4, 1, 0)
    a_y_got(2, 2, 0)
    a_y_got(2, 2, 1)
    b_x_got(6, 0)
    b_x_got(6, 1)
    z_got(0, 4, 0, 1)
    b_y_got(3, 0)
    core_send(0)
    a_y_got(0, 3, 0)
    z_got(1, 0, 1, 0)
    a_y_got(3, 2, 1)
    f_got(5)
    z_got(1, 0, 0, 0)
    a_y_got(3, 2, 0)
    a_y_got(1, 3, 0)
    z_got(1, 0, 1, 1)
    f_got(6)
    z_got(1, 0, 0, 1)
    a_y_got(2, 3, 0)
    scopies[0].wait_recv()
    b_x_got(7, 1)
    core_send(3)
    b_x_got(7, 0)
    core_send(2)
    z_got(0, 4, 1, 1)
    a_y_got(3, 3, 0)
    core_send(1)
    z_got(0, 5, 0, 0)
    z_got(1, 1, 1, 0)
    scopies[3].wait_recv()
    z_got(1, 1, 0, 0)
    f_got(7)
    core_send(4)
    scopies[2].wait_recv()
    z_got(1, 1, 1, 1)
    z_got(1, 1, 0, 1)
    z_got(0, 5, 1, 1)
    scopies[1].wait_recv()
    scopies[4].wait_recv()
    forward(0, 2)
    z_got(1, 2, 0, 0)
    z_got(1, 2, 1, 0)
    z_got(1, 2, 0, 1)
    forward(2, 4)
    z_got(1, 2, 1, 1)
    row_sums(0, act_ref, act_ref)
    sums_send(0, 0)
    turn(1, 0, 6)
    z_got(1, 3, 0, 0)
    z_got(1, 3, 1, 0)
    turn(1, 6, 12)
    turn(1, 12, 18)
    z_got(1, 3, 0, 1)
    z_got(1, 3, 1, 1)
    mid_ref[0] = sums_wait(0, 0)
    sums_send(0, 1)
    z_got(1, 4, 0, 0)
    z_got(1, 4, 1, 0)
    z_got(1, 4, 0, 1)
    z_got(1, 4, 1, 1)
    make_hidden(sums_wait(0, 1))
    gradient(1, 0, 2)
    z_got(1, 5, 0, 0)
    gradient(1, 2, 4)
    gradient(1, 4, 6)
    z_got(1, 5, 1, 1)
    deltas(1, 0)
    ring_part(1, 0, 0, 0)
    ring_part(1, 0, 1, 1)
    deltas(1, -1)
    deltas(1, 1)
    ring_part(1, 1, 1, 0)
    ring_part(1, 1, 0, 1)
    backward(0, 2)
    backward(2, 4)
    ring_part(1, 1, 1, 1)
    ring_part(1, 1, 0, 0)
    ring_part(1, 2, 0, 1)
    ring_part(1, 2, 1, 0)
    row_sums(1, back_ref, act_ref)
    sums_send(1, 0)
    deltas(1, -2)
    deltas(1, 2)
    ring_part(1, 2, 1, 1)
    deltas(1, 3)
    ring_part(1, 2, 0, 0)
    turn(0, 0, 6)
    mid_ref[1] = sums_wait(1, 0)
    sums_send(1, 1)
    ring_part(1, 3, 1, 0)
    ring_part(1, 3, 0, 1)
    turn(0, 6, 12)
    ring_part(1, 3, 1, 1)
    turn(0, 12, 18)
    ring_part(1, 3, 0, 0)
    make_dpre(sums_wait(1, 1))
    gradient(0, 0, 2)
    ring_part(1, 4, 1, 0)
    ring_part(1, 4, 0, 1)
    ring_part(1, 4, 1, 1)
    gradient(0, 2, 4)
    ring_part(1, 4, 0, 0)
    gradient(0, 4, 6)
    deltas(0, 0)
    ring_part(0, 0, 0, 0)
    ring_part(0, 0, 1, 1)
    ring_part(1, 5, 1, 0)
    ring_part(1, 5, 0, 1)
    deltas(0, -1)
    deltas(0, 1)
    ring_part(1, 5, 1, 1)
    ring_part(1, 5, 0, 0)
    ring_part(0, 1, 1, 0)
    ring_part(0, 1, 0, 1)
    deltas(0, -2)
    ring_part(0, 1, 1, 1)
    ring_part(0, 1, 0, 0)
    deltas(0, 2)
    deltas(0, 3)
    finish(1)
    ring_part(0, 2, 1, 0)
    ring_part(0, 2, 0, 1)
    ring_part(0, 2, 1, 1)
    ring_part(0, 2, 0, 0)
    ring_part(0, 3, 1, 0)
    ring_part(0, 3, 0, 1)
    outer(1)
    ring_part(0, 3, 1, 1)
    ring_part(0, 3, 0, 0)
    ring_part(0, 4, 1, 0)
    ring_part(0, 4, 0, 1)
    ring_part(0, 4, 1, 1)
    ring_part(0, 4, 0, 0)
    ring_part(0, 5, 1, 0)
    ring_part(0, 5, 0, 1)
    ring_part(0, 5, 1, 1)
    ring_part(0, 5, 0, 0)
    finish(0)
    outer(0)

    for copy in started:
        copy.wait_send()
    routed[1].wait_send()
    routed[2].wait_send()

    @pl.when(x != 0)
    def _():
        routed[0].wait_send()


VMEM = pl.BlockSpec(memory_space=pltpu.VMEM)
SMEM = pl.BlockSpec(memory_space=pltpu.SMEM)
DMA = pltpu.SemaphoreType.DMA


def fused(tokens, out_grad, slots, masters, members):
    shape = masters[0].shape
    sums = jax.ShapeDtypeStruct(shape, BF)
    return pl.pallas_call(
        fused_kernel,
        out_shape=(sums, sums),
        in_specs=[VMEM, VMEM, VMEM, VMEM, VMEM, SMEM],
        out_specs=(VMEM, VMEM),
        scratch_shapes=[
            pltpu.VMEM((2, 16, 512), F32),
            pltpu.VMEM((44, 4, 512), F32),
            pltpu.VMEM((192, HALF), BF),
            pltpu.VMEM((192, 2112), BF),
            pltpu.VMEM((192, HALF), BF),
            pltpu.VMEM((2, 4, BLOCK, 128), BF),
            pltpu.VMEM((2, 4, BLOCK, 128), BF),
            pltpu.VMEM((768, 704), BF),
            pltpu.VMEM((2, PLANE, WIDE), BF),
            pltpu.VMEM((2, WIDE, PLANE), BF),
            pltpu.VMEM((WIDE, 512), BF),
            pltpu.VMEM((WIDE, 512), BF),
            pltpu.VMEM((WIDE, 512), F32),
            pltpu.VMEM((WIDE, 512), BF),
            pltpu.VMEM((WIDE, 512), BF),
            pltpu.VMEM((PLANE, 128), F32),
            pltpu.VMEM((PLANE, 128), F32),
            pltpu.VMEM((PLANE, 128), F32),
            pltpu.VMEM((PLANE, 128), F32),
            pltpu.VMEM((PLANE, 512), BF),
            pltpu.VMEM((704, 768), BF),
            pltpu.VMEM((2, 4, BLOCK, 128), BF),
            pltpu.VMEM((2, 2, 6, USED, 512), BF),
            pltpu.VMEM((2, 4, BLOCK, 128), BF),
            pltpu.VMEM((2, 8, 128), F32),
            pltpu.VMEM((2, 8, 128), F32),
            pltpu.VMEM((2, 2, 8, 8, 128), F32),
            DMA((3, 2)),
            DMA((2, 3, 2)),
            DMA((2, 6, 2, 2, 2)),
            DMA((2, 6, 2, 2, 2)),
            DMA((3, 2)),
            DMA((4, 4, 2, 2)),
            DMA((4, 2, 2)),
            DMA((8, 2, 2)),
            DMA((8, 2)),
            DMA((5, 2)),
            DMA((2, 2, 7, 2)),
            DMA((2, 3, 2)),
            DMA,
        ],
        compiler_params=pltpu.CompilerParams(
            collective_id=0, has_side_effects=True, vmem_limit_bytes=56 * 1024 * 1024
        ),
        name="fused",
    )(tokens, out_grad, slots, *masters, members)


def on_device(
    tokens,
    out_grad,
    doc_lengths,
    doc_paths,
    membership,
    up_master,
    down_master,
    up_moment,
    down_moment,
):
    path_count = lax.axis_size("path")
    row_count = tokens.shape[0]
    capacity = row_count // path_count

    slots = row_slots(doc_lengths[0], doc_paths[0], row_count, path_count, capacity)

    def turned(array):
        return array.transpose(1, 0, 2)

    sums = fused(
        tokens, out_grad, slots[None, :], (turned(up_master), turned(down_master)), membership.T
    )
    module_ids = jnp.arange(up_master.shape[0], dtype=jnp.int32)

    def update(master, moment, level):
        counts = jnp.sum((membership[:, level][None, :] == module_ids[:, None]).astype(F32), axis=1)
        return outer_update(master, moment, turned(sums[level]).astype(F32), counts)

    new_up, new_up_moment = update(up_master, up_moment, 0)
    new_down, new_down_moment = update(down_master, down_moment, 1)
    return (new_up, new_down, new_up_moment, new_down_moment)


def solution(mesh):
    split = P(None, "path", "shard")
    rows = P("path", None)
    return jax.shard_map(
        on_device,
        mesh=mesh,
        in_specs=(rows, rows, rows, rows, P(), split, split, split, split),
        out_specs=(split, split, split, split),
        check_vma=False,
    )
```

```python
import functools

import jax
import jax.numpy as jnp
from jax import lax
from jax.experimental import pallas as pl
from jax.experimental.pallas import tpu as pltpu
from jax.sharding import PartitionSpec as P

MESH = pl.DeviceIdType.MESH
BF = jnp.bfloat16
F32 = jnp.float32

FF = 8192
NZ = 12
NYL = 4
NY = 8
NX = 4
UNIT = 16
HALF = 1152
WIDE = 2304
BLOCK = 192
USED = 176
PLANE = 768
PART = (96, 80)
OFFS = (0, -1, 1, -2, 2, -3, 3, -4)

norm_epsilon = 1e-06
hidden_epsilon = 1e-05
adam_epsilon = 0.001
inner_rate = 0.05
decay_rate = 0.1
outer_rate = 0.7
momentum_coef = 0.9
gelu_coef = 0.7978845608
cubic_coef = 0.044715


def gelu_pair(values):
    inner = gelu_coef * (values + cubic_coef * values * values * values)
    tangent = jnp.tanh(inner)
    activated = 0.5 * values * (1.0 + tangent)
    slopes = 0.5 * (1.0 + tangent) + 0.5 * values * (1.0 - tangent * tangent) * gelu_coef * (
        1.0 + 3.0 * cubic_coef * values * values
    )
    return (activated, slopes)


def row_slots(lengths, targets):
    docs = lengths.shape[1]
    before = (
        lax.broadcasted_iota(jnp.int32, (docs, docs), 0)
        <= lax.broadcasted_iota(jnp.int32, (docs, docs), 1)
    ).astype(F32)
    counts = jnp.broadcast_to(lengths, (8, docs)).astype(F32)
    paths = jnp.broadcast_to(targets, (8, docs)).astype(F32)
    ends = jnp.dot(counts.astype(BF), before.astype(BF), preferred_element_type=F32)[0:1, :]
    row = lax.broadcasted_iota(jnp.int32, (192, docs), 0).astype(F32)
    doc = lax.broadcasted_iota(jnp.int32, (192, docs), 1).astype(F32)
    doc_of_row = jnp.sum((row >= ends).astype(F32), axis=1, keepdims=True)
    hit = (doc_of_row == doc).astype(F32)
    path_column = jnp.sum(hit * paths[0:1, :], axis=1, keepdims=True)
    path_row = lax.dot_general(
        paths.astype(BF), hit.astype(BF), (((1,), (1,)), ((), ())), preferred_element_type=F32
    )[0:1, :]
    earlier = lax.broadcasted_iota(jnp.int32, (192, 192), 0) < lax.broadcasted_iota(
        jnp.int32, (192, 192), 1
    )
    same = jnp.where(earlier, (path_column == path_row).astype(F32), 0.0)
    rank = jnp.sum(same, axis=0, keepdims=True)
    return jnp.where(rank < 4.0, path_row * 4.0 + rank, -1.0)


def outer_update(master, moment, summed, counts):
    pseudo = -summed / jnp.maximum(counts, 1.0)[:, None, None]
    buffer = momentum_coef * moment.astype(jnp.float32) + pseudo
    return (master - outer_rate * (pseudo + momentum_coef * buffer), buffer.astype(jnp.bfloat16))


def place():
    path = lax.axis_index("path")
    shard = lax.axis_index("shard")
    return path // NYL, path % NYL, shard // 8, (shard // 2) % NX, shard % 2


def device(z, y, x, core):
    return (z * NYL + y % NYL, ((y // NYL) * NX + x) * 2 + core)


def aligned(value, multiple):
    return pl.multiple_of(value, multiple)


def signal(to):
    pl.semaphore_signal(
        pltpu.get_barrier_semaphore(), inc=1, device_id=to, device_id_type=MESH
    )


def fused_kernel(
    tokens,
    out_grad,
    lengths_ref,
    targets_ref,
    up_master,
    down_master,
    member_ref,
    up_sums,
    down_sums,
    mask_ref,
    total_ref,
    padded,
    chosen_ref,
    blocks_ref,
    wsend_ref,
    landed,
    back_perm,
    xs,
    xt,
    up_w,
    down_w,
    grads,
    up_p,
    down_p,
    act_ref,
    slope_ref,
    back_ref,
    scale_ref,
    spread_ref,
    perm_ref,
    wrecv,
    recv,
    work,
    sums_ref,
    mid_ref,
    slots,
    a_sem,
    e_sem,
    z_sem,
    r_sem,
    ax_sem,
    ay_sem,
    by_sem,
    bx_sem,
    f_sem,
    s_sem,
    t_sem,
    o_sem,
    l_sem,
):
    z, y_lo, y_hi, x, core = place()
    y = y_hi * NYL + y_lo
    c = x * 2 + core
    weights = (up_w, down_w)
    masters = (up_master, down_master)
    outputs = (up_sums, down_sums)
    parts = (up_p, down_p)

    def remote(src, dst, sems, to):
        return pltpu.make_async_remote_copy(
            src_ref=src,
            dst_ref=dst,
            send_sem=sems.at[0],
            recv_sem=sems.at[1],
            device_id=to,
            device_id_type=MESH,
        )

    started = []

    def start(src, dst, sems, to):
        copy = remote(src, dst, sems, to)
        copy.start()
        started.append(copy)
        return copy

    x_right, x_left, x_far = (x + 1) % NX, (x + 3) % NX, (x + 2) % NX
    to_x = (device(z, y, x_right, core), device(z, y, x_left, core))
    to_y = (device(z, (y + 1) % NY, x, core), device(z, (y + 7) % NY, x, core))
    to_z = (device((z + 1) % NZ, y, x, core), device((z + 11) % NZ, y, x, core))
    to_core = device(z, y, x, 1 - core)
    all_y = [device(z, (y + s) % NY, x, core) for s in range(1, NY)]
    all_c = [device(z, y, ((c + s) % 8) // 2, (c + s) % 2) for s in range(1, 8)]

    for to in all_y + all_c:
        signal(to)
    for to in to_z:
        signal(to)
    hops = [
        jnp.where(x == 0, a, jnp.where(x == 1, b, jnp.where(x == 2, c_, d)))
        for a, b, c_, d in ((0, 1, 2, 6), (5, 4, 3, 9), (7, 8, 11, 10))
    ]
    signal(device((z + NZ - jnp.where(x == 0, 6, hops[0])) % NZ, y, x, core))
    for j in (1, 2):
        signal(device((z + NZ - hops[j]) % NZ, y, x, core))
    for level in range(2):
        for other in range(4):
            for m in range(4):
                wsend_ref[level, other, m * 48 + 32 : m * 48 + 48, :] = jnp.zeros((16, 128), BF)
    for level in range(2):
        for m in range(4):
            values = masters[level][:, m, :].astype(BF)
            for other in range(4):
                wsend_ref[level, other, m * 48 : m * 48 + 44, :] = values[
                    :, other * 128 : (other + 1) * 128
                ]
    rows_float = tokens[...].astype(F32)
    normed = (
        rows_float
        * lax.rsqrt(jnp.mean(rows_float * rows_float, axis=1, keepdims=True) + norm_epsilon)
    ).astype(BF)
    chosen_ref[...] = jnp.where(core == 0, normed, out_grad[...])
    blocks_ref[...] = jnp.zeros_like(blocks_ref)
    for n in range(NZ // 2):
        low = chosen_ref[:, n * USED : (n + 1) * USED]
        high = chosen_ref[:, (n + 6) * USED : (n + 7) * USED]
        blocks_ref[:, n * BLOCK : n * BLOCK + USED] = jnp.where(y_hi == 0, low, high)
    placing = (
        lax.broadcasted_iota(jnp.int32, (192, 192), 0).astype(F32)
        == row_slots(lengths_ref[...], targets_ref[...])
    ).astype(F32)
    padded[...] = jnp.dot(
        placing.astype(BF), blocks_ref[...], preferred_element_type=F32
    ).astype(BF)
    pl.semaphore_wait(pltpu.get_barrier_semaphore(), 19)

    half_cols = pl.ds(aligned(y_hi * HALF, 128), HALF)

    def trade_columns(level):
        copies = []
        for step in (1, 2, 3):
            other = (y_lo + step) % NYL
            copies.append(
                start(
                    wsend_ref.at[level, other],
                    wrecv.at[level, y_lo],
                    e_sem.at[level, step - 1],
                    device(z, y_hi * NYL + other, x, core),
                )
            )
        wrecv[level, y_lo] = wsend_ref[level, y_lo]
        return copies

    trades = [trade_columns(0)]
    b_row = 256 + (x * NYL + y_lo) * 32
    landing = [
        xs.at[core, pl.ds(aligned((y_lo * NX + x) * UNIT, 16), UNIT), half_cols],
        xs.at[core, pl.ds(aligned(b_row, 16), UNIT), half_cols],
        xs.at[core, pl.ds(aligned(b_row + UNIT, 16), UNIT), half_cols],
    ]
    routed = []
    for j in range(3):
        target = (z + hops[j]) % NZ
        routed.append(
            remote(
                padded.at[pl.ds(aligned(target * UNIT, 16), UNIT), :],
                landing[j],
                a_sem.at[j],
                device(target, y, x, core),
            )
        )
    own_rows = pltpu.make_async_copy(
        padded.at[pl.ds(aligned(z * UNIT, 16), UNIT), :], landing[0], l_sem
    )
    routed[1].start()
    routed[2].start()

    @pl.when(x == 0)
    def _():
        own_rows.start()

    @pl.when(x != 0)
    def _():
        routed[0].start()

    for level in range(2):
        for zz in range(NZ):
            weights[level][zz * BLOCK + USED : (zz + 1) * BLOCK, :] = jnp.zeros(
                (BLOCK - USED, 512), BF
            )
    sums_ref[...] = jnp.zeros_like(sums_ref)
    choice = [
        [
            [jnp.where(member_ref[level, z * NYL + i] == m, 1.0, 0.0) for m in range(4)]
            for i in range(4)
        ]
        for level in range(2)
    ]
    path_of_row = lax.broadcasted_iota(jnp.int32, (16, 128), 0) // 4
    for level in range(2):
        for m in range(4):
            mask_ref[level, :, m * 128 : (m + 1) * 128] = sum(
                jnp.where(path_of_row == i, choice[level][i][m], 0.0) for i in range(4)
            )

    def fill_perm(i, carry):
        here = pl.ds(aligned(i * 16, 16), 16)
        a = lax.broadcasted_iota(jnp.int32, (16, 1), 0) + i * 16
        b = lax.broadcasted_iota(jnp.int32, (16, 768), 1)
        first = sum((a >= 176 * n).astype(jnp.int32) for n in (1, 2, 3))
        rest = a - 176 * first
        second = sum((rest >= 44 * n).astype(jnp.int32) for n in (1, 2, 3))
        to_b = second * 192 + first * 48 + rest - 44 * second
        perm_ref[here, :] = jnp.where(b == to_b, 1.0, 0.0).astype(BF)
        return carry

    def fill_back(i, carry):
        here = pl.ds(aligned(i * 16, 16), 16)
        b = lax.broadcasted_iota(jnp.int32, (16, 1), 0) + i * 16
        a = lax.broadcasted_iota(jnp.int32, (16, 704), 1)
        first = sum((b >= 192 * n).astype(jnp.int32) for n in (1, 2, 3))
        rest = b - 192 * first
        second = sum((rest >= 48 * n).astype(jnp.int32) for n in (1, 2, 3))
        row = rest - 48 * second
        to_a = jnp.where(row < 44, second * 176 + first * 44 + row, -1)
        back_perm[here, :] = jnp.where(a == to_a, 1.0, 0.0).astype(BF)
        return carry

    def constants():
        lax.fori_loop(0, 48, fill_back, 0)

    lax.fori_loop(0, 44, fill_perm, 0)

    zcopies = {}

    def wblock(level, zz, h):
        return weights[level].at[
            pl.ds(aligned(zz * BLOCK, 16), USED), h * 256 : (h + 1) * 256
        ]

    def z_send(level, t, side, h):
        zz = (z + NZ + (-t if side == 0 else t)) % NZ
        dst = wblock(level, zz, h)
        zcopies[level, t, side, h] = start(dst, dst, z_sem.at[level, t, side, h], to_z[side])

    def z_first(level):
        for copy in trades[level]:
            copy.wait_recv()
        pieces = wrecv[level].reshape(4 * BLOCK, 128)
        for m in range(4):
            weights[level][pl.ds(aligned(z * BLOCK, 16), USED), m * 128 : (m + 1) * 128] = jnp.dot(
                perm_ref[m * USED : (m + 1) * USED, :], pieces, preferred_element_type=F32
            ).astype(BF)
        for h in range(2):
            for side in range(2):
                z_send(level, 0, side, h)

    def z_got(level, t, side, h):
        zcopies[level, t, side, h].wait_recv()
        if t < 4 or (t == 4 and h == side):
            z_send(level, t + 1, side, h)

    def a_unit(xx):
        return a_part(xx, y)

    def cols_of(yy):
        return pl.ds(aligned((yy // NYL) * HALF, 128), HALF)

    def a_part(xx, yy):
        return xs.at[
            core, pl.ds(aligned(((yy % NYL) * NX + xx) * UNIT, 16), UNIT), cols_of(yy)
        ]

    def b_chunk(xx, yy):
        return xs.at[
            core, pl.ds(aligned(256 + (xx * NYL + yy % NYL) * 32, 16), 32), cols_of(yy)
        ]

    def b_slab(xx):
        return xs.at[core, pl.ds(aligned(256 + xx * 128, 16), 128), :]

    ycopies = {}

    def y_send(name, block, sems, t, side):
        ref = block((y + NY + (-t if side == 0 else t)) % NY)
        ycopies[name, t, side] = start(ref, ref, sems.at[t, side], to_y[side])

    def b_y_send(t, side):
        y_send("b", lambda yy: b_chunk(x, yy), by_sem, t, side)

    def a_y_send(k, t, side):
        y_send(k, lambda yy: a_part(lanes_a[k], yy), ay_sem.at[k], t, side)

    def onward(t, side):
        return t < 3 and (side == 0 or t < 2)

    lanes_a = (x, x_left, x_right, x_far)
    xcopies = {}
    fcopies = {}
    acopies = {}
    scopies = []

    def b_x_send(n):
        ref = b_chunk(x, (y + NY + OFFS[n]) % NY)
        for side in range(2):
            xcopies[n, side] = start(ref, ref, bx_sem.at[n, side], to_x[side])

    def core_send(index):
        ref = xs.at[core, pl.ds(0, 256), :] if index == 1 else b_slab((x, x, x_left, x_right, x_far)[index])
        scopies.append(start(ref, ref, s_sem.at[len(scopies)], to_core))

    def rows_got():
        routed[1].wait_recv()
        routed[2].wait_recv()
        b_y_send(0, 0)
        b_y_send(0, 1)

        @pl.when(x == 0)
        def _():
            own_rows.wait()

        @pl.when(x != 0)
        def _():
            routed[0].wait_recv()

        own = a_unit(x)
        for side in range(2):
            acopies[side] = start(own, own, ax_sem.at[side], to_x[side])
        a_y_send(0, 0, 0)
        a_y_send(0, 0, 1)
        b_x_send(0)

    def a_x_got(i):
        acopies[i].wait_recv()
        if i == 0:
            passed = a_unit(x_left)
            acopies[2] = start(passed, passed, ax_sem.at[2], to_x[0])
        a_y_send(i + 1, 0, 0)
        a_y_send(i + 1, 0, 1)

    def b_y_got(t, side):
        ycopies["b", t, side].wait_recv()
        if onward(t, side):
            b_y_send(t + 1, side)
        b_x_send(2 * t + 1 + side)

    def a_y_got(k, t, side):
        ycopies[k, t, side].wait_recv()
        if onward(t, side):
            a_y_send(k, t + 1, side)

    def b_x_got(n, side):
        xcopies[n, side].wait_recv()
        if n % 2 == side:
            ref = b_chunk((x_left, x_right)[side], (y + NY + OFFS[n]) % NY)
            fcopies[n] = start(ref, ref, f_sem.at[n], to_x[side])

    def f_got(n):
        fcopies[n].wait_recv()

    tcopies = {}

    def sums_send(which, stage):
        src = (sums_ref, mid_ref)[stage].at[which]
        mine = (y, c)[stage]
        tcopies[which, stage] = [
            start(src, slots.at[which, stage, mine], t_sem.at[which, stage, s], to)
            for s, to in enumerate((all_y, all_c)[stage])
        ]
        slots[which, stage, mine] = src[...]

    def sums_wait(which, stage):
        for copy in tcopies[which, stage]:
            copy.wait_recv()
        total = slots[which, stage, 0]
        for i in range(1, 8):
            total += slots[which, stage, i]
        return total

    def picked(product, level):
        masked = product.reshape(12, 16, 512) * mask_ref[level][None]
        total = masked[:, :, :128]
        for m in range(1, 4):
            total = total + masked[:, :, m * 128 : (m + 1) * 128]
        return total.reshape(BLOCK, 128)

    def forward(first, last):
        def body(i, carry):
            here = pl.ds(aligned(i * BLOCK, 16), BLOCK)
            pre = picked(jnp.dot(xs[0, here, :], up_w[...], preferred_element_type=F32), 0)
            act_ref[here, :], slope_ref[here, :] = gelu_pair(pre)
            return carry

        lax.fori_loop(first, last, body, 0)

    def backward(first, last):
        def body(i, carry):
            here = pl.ds(aligned(i * BLOCK, 16), BLOCK)
            back_ref[here, :] = picked(
                jnp.dot(xs[1, here, :], down_w[...], preferred_element_type=F32), 1
            )
            return carry

        lax.fori_loop(first, last, body, 0)

    def row_sums(which, left, right):
        for k in range(6):
            here = slice(k * 128, (k + 1) * 128)
            sums_ref[which, k : k + 1, :] = jnp.sum(
                (left[here, :] * right[here, :]).T, axis=0, keepdims=True
            )

    def column(row):
        return jnp.broadcast_to(row, (128, 128)).T

    def store_spread(k, values):
        here = slice(k * 128, (k + 1) * 128)
        path = (lax.broadcasted_iota(jnp.int32, (128, 128), 0) // 4) % 4
        for i in range(4):
            spread_ref[here, i * 128 : (i + 1) * 128] = jnp.where(path == i, values, 0.0).astype(BF)

    def make_hidden(total):
        scale_row = jnp.sqrt(total / FF + hidden_epsilon)
        for k in range(6):
            here = slice(k * 128, (k + 1) * 128)
            scale = column(scale_row[k : k + 1, :])
            scale_ref[here, :] = scale
            hidden = act_ref[here, :] / scale
            act_ref[here, :] = hidden
            store_spread(k, hidden)

    def make_dpre(total):
        mix_row = total / FF
        for k in range(6):
            here = slice(k * 128, (k + 1) * 128)
            mixing = column(mix_row[k : k + 1, :])
            hidden = act_ref[here, :]
            store_spread(
                k,
                (back_ref[here, :] - hidden * mixing) / scale_ref[here, :] * slope_ref[here, :],
            )

    def turn(which, first, last):
        def body(i, carry):
            here = pl.ds(aligned(i * 128, 128), 128)
            xt[which, here, :] = xs[which, :, here].T
            return carry

        lax.fori_loop(first, last, body, 0)

    def gradient(which, first, last):
        def body(i, carry):
            here = pl.ds(aligned(i * 384, 128), 384)
            grads[here, :] = jnp.dot(
                xt[which, here, :], spread_ref[...], preferred_element_type=F32
            )
            return carry

        lax.fori_loop(first, last, body, 0)

    q_first = ((z + 6) % NZ) // 2

    def deltas(level, offset):
        base = ((q_first + 6 + offset) % 6) * 384
        chosen = choice[level]
        members = [member_ref[level, z * NYL + i] for i in range(4)]

        def body(i, carry):
            here = pl.ds(aligned(base + i * 32, 32), 32)
            modules = [weights[level][here, m * 128 : (m + 1) * 128] for m in range(4)]
            totals = [None] * 4
            for p in range(4):
                gradient_p = grads[here, p * 128 : (p + 1) * 128]
                weight_p = modules[0]
                for m in range(1, 4):
                    weight_p = jnp.where(members[p] == m, modules[m], weight_p)
                weight_p = weight_p.astype(F32)
                size = jnp.abs(gradient_p) + adam_epsilon
                inverse = pl.reciprocal(size, approx=True)
                inverse = inverse * (2.0 - size * inverse)
                update = gradient_p * inverse + decay_rate * weight_p
                delta = (-inner_rate * update).astype(BF).astype(F32)
                for m in range(4):
                    term = chosen[p][m] * delta
                    totals[m] = term if p == 0 else totals[m] + term
            for m in range(4):
                parts[level][here, m * 128 : (m + 1) * 128] = totals[m].astype(BF)
            return carry

        lax.fori_loop(0, 12, body, 0)

    rcopies = {}

    def pblock(level, zz, h):
        return parts[level].at[
            pl.ds(aligned(zz * BLOCK + 96 * h, 16), PART[h]), :
        ]

    def held_part(level, side, t, h):
        return recv.at[level, side, t, 96 * h : 96 * h + PART[h], :]

    def ring_part(level, t, side, h):
        zz = (z + (6 - t if side == 0 else NZ - 6 + t)) % NZ
        src = pblock(level, zz, h)
        if (level, t - 1, side, h) in rcopies:
            rcopies[level, t - 1, side, h].wait_recv()
            held = held_part(level, side, t - 1, h)
            held[...] = held[...] + src[...]
            src = held
        rcopies[level, t, side, h] = start(
            src, held_part(level, side, t, h), r_sem.at[level, t, side, h], to_z[side]
        )

    ocopies = {}

    def finish(level):
        totals = []
        for h in range(2):
            for side in range(2):
                rcopies[level, 5, side, h].wait_recv()
            totals.append(
                pblock(level, z, h)[...].astype(F32)
                + held_part(level, 0, 5, h)[...].astype(F32)
                + held_part(level, 1, 5, h)[...].astype(F32)
            )
        total = jnp.concatenate(totals, axis=0).astype(BF)
        pieces = [total[:, m * 128 : (m + 1) * 128] for m in range(4)]
        work[level] = (
            jnp.dot(back_perm[...], jnp.concatenate(pieces, axis=0), preferred_element_type=F32)
            .astype(BF)
            .reshape(4, BLOCK, 128)
        )
        for step in (1, 2, 3):
            other = (y_lo + step) % NYL
            ocopies[level, step] = start(
                work.at[level, other],
                landed.at[level, y_lo],
                o_sem.at[level, step - 1],
                device(z, y_hi * NYL + other, x, core),
            )
        landed[level, y_lo] = work[level, y_lo]

    def outer(level):
        for step in (1, 2, 3):
            ocopies[level, step].wait_recv()
        for m in range(4):
            total_ref[:, m, :] = jnp.concatenate(
                [landed[level, n, m * 48 : m * 48 + 44, :].astype(F32) for n in range(4)], axis=1
            )
        outputs[level][...] = total_ref[...].astype(BF)

    z_first(0)
    constants()
    rows_got()
    z_got(0, 0, 0, 0)
    z_got(0, 0, 1, 0)
    a_x_got(0)
    a_x_got(1)
    b_y_got(0, 0)
    z_got(0, 0, 0, 1)
    b_y_got(0, 1)
    z_got(0, 0, 1, 1)
    a_y_got(0, 0, 0)
    a_y_got(0, 0, 1)
    b_x_got(0, 0)
    b_x_got(0, 1)
    a_x_got(2)
    z_got(0, 1, 0, 0)
    a_y_got(1, 0, 0)
    z_got(0, 1, 1, 0)
    a_y_got(1, 0, 1)
    a_y_got(2, 0, 0)
    a_y_got(2, 0, 1)
    b_x_got(1, 0)
    b_x_got(1, 1)
    z_got(0, 1, 0, 1)
    b_y_got(1, 0)
    trades.append(trade_columns(1))
    b_y_got(1, 1)
    a_y_got(0, 1, 0)
    z_got(0, 1, 1, 1)
    a_y_got(0, 1, 1)
    b_x_got(2, 0)
    b_x_got(2, 1)
    a_y_got(3, 0, 0)
    a_y_got(3, 0, 1)
    a_y_got(1, 1, 0)
    a_y_got(1, 1, 1)
    f_got(0)
    z_got(0, 2, 0, 0)
    z_got(0, 2, 1, 0)
    a_y_got(2, 1, 0)
    a_y_got(2, 1, 1)
    f_got(1)
    z_got(0, 2, 0, 1)
    b_x_got(3, 0)
    b_y_got(2, 0)
    b_x_got(3, 1)
    b_x_got(4, 0)
    z_got(0, 2, 1, 1)
    b_x_got(4, 1)
    f_got(2)
    z_got(0, 3, 0, 0)
    z_first(1)
    z_got(0, 3, 1, 0)
    b_y_got(2, 1)
    a_y_got(0, 2, 0)
    b_x_got(5, 0)
    a_y_got(0, 2, 1)
    b_x_got(5, 1)
    a_y_got(3, 1, 0)
    z_got(0, 3, 0, 1)
    a_y_got(3, 1, 1)
    z_got(0, 3, 1, 1)
    a_y_got(1, 2, 0)
    f_got(4)
    a_y_got(1, 2, 1)
    f_got(3)
    a_y_got(2, 2, 0)
    a_y_got(2, 2, 1)
    b_y_got(3, 0)
    core_send(0)
    z_got(0, 4, 0, 0)
    a_y_got(0, 3, 0)
    z_got(1, 0, 1, 0)
    b_x_got(6, 0)
    b_x_got(6, 1)
    a_y_got(3, 2, 0)
    z_got(1, 0, 0, 0)
    a_y_got(3, 2, 1)
    a_y_got(1, 3, 0)
    z_got(1, 0, 1, 1)
    f_got(5)
    a_y_got(2, 3, 0)
    z_got(1, 0, 0, 1)
    scopies[0].wait_recv()
    b_x_got(7, 0)
    core_send(2)
    b_x_got(7, 1)
    core_send(3)
    z_got(0, 4, 1, 0)
    a_y_got(3, 3, 0)
    core_send(1)
    z_got(0, 4, 0, 1)
    f_got(6)
    z_got(0, 4, 1, 1)
    z_got(0, 5, 0, 0)
    scopies[2].wait_recv()
    z_got(1, 1, 1, 0)
    f_got(7)
    core_send(4)
    scopies[3].wait_recv()
    z_got(1, 1, 0, 0)
    z_got(1, 1, 1, 1)
    scopies[1].wait_recv()
    z_got(1, 1, 0, 1)
    z_got(0, 5, 1, 1)
    scopies[4].wait_recv()
    forward(0, 1)
    forward(1, 2)
    z_got(1, 2, 0, 0)
    z_got(1, 2, 1, 0)
    forward(2, 3)
    forward(3, 4)
    z_got(1, 2, 0, 1)
    z_got(1, 2, 1, 1)
    row_sums(0, act_ref, act_ref)
    sums_send(0, 0)
    turn(1, 0, 6)
    z_got(1, 3, 0, 0)
    z_got(1, 3, 1, 0)
    turn(1, 6, 12)
    turn(1, 12, 18)
    z_got(1, 3, 0, 1)
    z_got(1, 3, 1, 1)
    mid_ref[0] = sums_wait(0, 0)
    sums_send(0, 1)
    z_got(1, 4, 0, 0)
    z_got(1, 4, 1, 0)
    z_got(1, 4, 0, 1)
    z_got(1, 4, 1, 1)
    make_hidden(sums_wait(0, 1))
    gradient(1, 0, 1)
    gradient(1, 1, 2)
    gradient(1, 2, 3)
    z_got(1, 5, 0, 0)
    gradient(1, 3, 4)
    gradient(1, 4, 5)
    gradient(1, 5, 6)
    z_got(1, 5, 1, 1)
    deltas(1, 0)
    ring_part(1, 0, 0, 0)
    ring_part(1, 0, 1, 1)
    deltas(1, -1)
    deltas(1, 1)
    ring_part(1, 1, 1, 0)
    ring_part(1, 1, 0, 1)
    backward(0, 1)
    backward(1, 2)
    backward(2, 3)
    backward(3, 4)
    ring_part(1, 1, 1, 1)
    ring_part(1, 1, 0, 0)
    row_sums(1, back_ref, act_ref)
    sums_send(1, 0)
    ring_part(1, 2, 0, 1)
    ring_part(1, 2, 1, 0)
    deltas(1, -2)
    deltas(1, 2)
    deltas(1, 3)
    ring_part(1, 2, 1, 1)
    ring_part(1, 2, 0, 0)
    mid_ref[1] = sums_wait(1, 0)
    sums_send(1, 1)
    turn(0, 0, 6)
    ring_part(1, 3, 0, 1)
    ring_part(1, 3, 1, 0)
    turn(0, 6, 12)
    turn(0, 12, 18)
    ring_part(1, 3, 1, 1)
    ring_part(1, 3, 0, 0)
    make_dpre(sums_wait(1, 1))
    gradient(0, 0, 1)
    ring_part(1, 4, 0, 1)
    gradient(0, 1, 2)
    ring_part(1, 4, 1, 0)
    gradient(0, 2, 3)
    gradient(0, 3, 4)
    ring_part(1, 4, 1, 1)
    ring_part(1, 4, 0, 0)
    gradient(0, 4, 5)
    gradient(0, 5, 6)
    deltas(0, 0)
    ring_part(1, 5, 0, 1)
    ring_part(0, 0, 0, 0)
    ring_part(0, 0, 1, 1)
    deltas(0, -1)
    ring_part(1, 5, 1, 0)
    deltas(0, 1)
    ring_part(0, 1, 1, 0)
    ring_part(0, 1, 0, 1)
    deltas(0, -2)
    ring_part(1, 5, 1, 1)
    ring_part(1, 5, 0, 0)
    deltas(0, 2)
    deltas(0, 3)
    ring_part(0, 1, 1, 1)
    ring_part(0, 1, 0, 0)
    ring_part(0, 2, 0, 1)
    ring_part(0, 2, 1, 0)
    finish(1)
    ring_part(0, 2, 1, 1)
    ring_part(0, 2, 0, 0)
    ring_part(0, 3, 0, 1)
    ring_part(0, 3, 1, 0)
    ring_part(0, 3, 1, 1)
    ring_part(0, 3, 0, 0)
    outer(1)
    ring_part(0, 4, 0, 1)
    ring_part(0, 4, 1, 0)
    ring_part(0, 4, 1, 1)
    ring_part(0, 4, 0, 0)
    ring_part(0, 5, 0, 1)
    ring_part(0, 5, 1, 0)
    ring_part(0, 5, 1, 1)
    ring_part(0, 5, 0, 0)
    finish(0)
    outer(0)

    for copy in started:
        copy.wait_send()
    routed[1].wait_send()
    routed[2].wait_send()

    @pl.when(x != 0)
    def _():
        routed[0].wait_send()


VMEM = pl.BlockSpec(memory_space=pltpu.VMEM)
SMEM = pl.BlockSpec(memory_space=pltpu.SMEM)
DMA = pltpu.SemaphoreType.DMA


def fused(tokens, out_grad, lengths, targets, masters, members):
    shape = masters[0].shape
    sums = jax.ShapeDtypeStruct(shape, BF)
    return pl.pallas_call(
        fused_kernel,
        out_shape=(sums, sums),
        in_specs=[VMEM, VMEM, VMEM, VMEM, VMEM, VMEM, SMEM],
        out_specs=(VMEM, VMEM),
        scratch_shapes=[
            pltpu.VMEM((2, 16, 512), F32),
            pltpu.VMEM((44, 4, 512), F32),
            pltpu.VMEM((192, HALF), BF),
            pltpu.VMEM((192, 2112), BF),
            pltpu.VMEM((192, HALF), BF),
            pltpu.VMEM((2, 4, BLOCK, 128), BF),
            pltpu.VMEM((2, 4, BLOCK, 128), BF),
            pltpu.VMEM((768, 704), BF),
            pltpu.VMEM((2, PLANE, WIDE), BF),
            pltpu.VMEM((2, WIDE, PLANE), BF),
            pltpu.VMEM((WIDE, 512), BF),
            pltpu.VMEM((WIDE, 512), BF),
            pltpu.VMEM((WIDE, 512), F32),
            pltpu.VMEM((WIDE, 512), BF),
            pltpu.VMEM((WIDE, 512), BF),
            pltpu.VMEM((PLANE, 128), F32),
            pltpu.VMEM((PLANE, 128), F32),
            pltpu.VMEM((PLANE, 128), F32),
            pltpu.VMEM((PLANE, 128), F32),
            pltpu.VMEM((PLANE, 512), BF),
            pltpu.VMEM((704, 768), BF),
            pltpu.VMEM((2, 4, BLOCK, 128), BF),
            pltpu.VMEM((2, 2, 6, USED, 512), BF),
            pltpu.VMEM((2, 4, BLOCK, 128), BF),
            pltpu.VMEM((2, 8, 128), F32),
            pltpu.VMEM((2, 8, 128), F32),
            pltpu.VMEM((2, 2, 8, 8, 128), F32),
            DMA((3, 2)),
            DMA((2, 3, 2)),
            DMA((2, 6, 2, 2, 2)),
            DMA((2, 6, 2, 2, 2)),
            DMA((3, 2)),
            DMA((4, 4, 2, 2)),
            DMA((4, 2, 2)),
            DMA((8, 2, 2)),
            DMA((8, 2)),
            DMA((5, 2)),
            DMA((2, 2, 7, 2)),
            DMA((2, 3, 2)),
            DMA,
        ],
        compiler_params=pltpu.CompilerParams(
            collective_id=0, has_side_effects=True, vmem_limit_bytes=56 * 1024 * 1024
        ),
        name="fused",
    )(tokens, out_grad, lengths, targets, *masters, members)


def on_device(
    tokens,
    out_grad,
    doc_lengths,
    doc_paths,
    membership,
    up_master,
    down_master,
    up_moment,
    down_moment,
):
    def turned(array):
        return array.transpose(1, 0, 2)

    sums = fused(
        tokens,
        out_grad,
        doc_lengths,
        doc_paths,
        (turned(up_master), turned(down_master)),
        membership.T,
    )
    module_ids = jnp.arange(up_master.shape[0], dtype=jnp.int32)

    def update(master, moment, level):
        counts = jnp.sum((membership[:, level][None, :] == module_ids[:, None]).astype(F32), axis=1)
        return outer_update(master, moment, turned(sums[level]).astype(F32), counts)

    new_up, new_up_moment = update(up_master, up_moment, 0)
    new_down, new_down_moment = update(down_master, down_moment, 1)
    return (new_up, new_down, new_up_moment, new_down_moment)


def solution(mesh):
    split = P(None, "path", "shard")
    rows = P("path", None)
    return jax.shard_map(
        on_device,
        mesh=mesh,
        in_specs=(rows, rows, rows, rows, P(), split, split, split, split),
        out_specs=(split, split, split, split),
        check_vma=False,
    )
```
